32 devices in a mesh: row: 16 (over z, y, core), chan: 2 (over x).
Axes of the slice: x: 2, y: 2, z: 4, core: 2. Of those that a mesh axis runs over, the one named last changes fastest.
Arguments:
- pair: float32 [128, 32, 32], P('chan', 'row'), may hold values from -6 to 6
- in_gain: float32 [128], replicated, may hold values from 0.1 to 1.9
- output_gain: float32 [128], P('chan'), may hold values from 0.1 to 1.9
- w_edges: float32 [4, 128, 128], P(None, None, 'chan'), may hold values from -0.5 to 0.5
- w_gate: float32 [128, 128], P(None, 'chan'), may hold values from -0.5 to 0.5
- w_out: float32 [128, 128], P('chan'), may hold values from -0.5 to 0.5
- cotangent: float32 [128, 32, 32], P('chan', 'row'), may hold values from -6 to 6
Outputs:
- update: float32 [128, 32, 32], P('chan', 'row')
- d_pair: float32 [128, 32, 32], P('chan', 'row')
- d_in_gain: float32 [128], P('chan')
- d_out_gain: float32 [128], P('chan')
- d_edges: float32 [4, 128, 128], P(None, None, 'chan')
- d_gate: float32 [128, 128], P(None, 'chan')
- d_out: float32 [128, 128], P('chan')
The draws below stay inside these ranges and needn't reach their ends.
All inputs are finite; a program needn't handle non-finite values.
Results may differ from the reference program's by a relative error of at most 0.00019.
Values sent between devices are 32-bit elements; how exact they have to be, the bound alone decides.
No kernel may reach another device: no remote copies, remote signals or barrier semaphores. Data moves between devices by JAX's collectives and lax.ppermute only.
A program may use at most 64 MiB of HBM per device.

```python
import jax
import jax.numpy as jnp
from jax import lax

C = 128
HIDDEN_WIDTH = 128
N = 32


def steps_of(own_key, dims, pieces, low, high):
    def one(dim, blocks):
        draws = jax.random.uniform(jax.random.fold_in(jax.random.fold_in(own_key, 6), dim), (blocks,), jnp.float32, low / len(pieces), high / len(pieces))
        return jnp.repeat(jnp.exp(draws), dims[dim] // blocks).reshape((-1,) + (1,) * (len(dims) - dim - 1))

    factor_of = one(*pieces[0])
    for cut in pieces[1:]:
        factor_of = factor_of * one(*cut)
    return factor_of


def bell_draw(rng, shape, scale, reach, split=(), dtype=jnp.bfloat16):
    level = steps_of(rng, shape, split, -0.22, 0.18) if split else 1.0
    entries = jax.random.normal(rng, shape, jnp.float32) * scale * level
    return jnp.minimum(jnp.maximum(entries, -reach), reach).astype(dtype)


def setup_inputs(seed: int = 0) -> dict:
    splits = jax.random.split(jax.random.key(seed), 8)
    pair = bell_draw(splits[0], (C, N, N), 1.0, 6.0, ((0, 2), (1, 16)), jnp.float32)
    in_gain = jnp.clip(1.0 + 0.18 * jax.random.normal(splits[1], (C,), jnp.float32), 0.1, 1.9)
    output_gain = jnp.clip(1.0 + 0.18 * jax.random.normal(splits[2], (HIDDEN_WIDTH,), jnp.float32), 0.1, 1.9)
    w_edges = bell_draw(splits[3], (4, C, HIDDEN_WIDTH), C ** -0.5, 0.5, ((2, 2),), jnp.float32)
    w_gate = bell_draw(splits[4], (C, C), C ** -0.5, 0.5, ((1, 2),), jnp.float32)
    w_out = bell_draw(splits[5], (HIDDEN_WIDTH, C), HIDDEN_WIDTH ** -0.5, 0.5, ((0, 2),), jnp.float32)
    cotangent = bell_draw(splits[6], (C, N, N), 1.0, 6.0, ((0, 2), (1, 16)), jnp.float32)
    return {"pair": pair, "in_gain": in_gain, "output_gain": output_gain, "w_edges": w_edges, "w_gate": w_gate, "w_out": w_out, "cotangent": cotangent}


def channel_norm(values, gain):
    mean = lax.optimization_barrier(jnp.mean(values, 0))
    centred = values - mean
    var = lax.optimization_barrier(jnp.mean(centred * centred, 0))
    return centred * lax.rsqrt(var + 1e-05) * gain[:, None, None]

def forward(pair, in_gain, output_gain, w_edges, w_gate, w_out):
    hp = lax.Precision.HIGHEST
    normed = channel_norm(pair, in_gain)
    proj = jnp.einsum('ech,cin->ehin', w_edges, normed, precision=hp)
    left = jax.nn.sigmoid(proj[1]) * proj[0]
    right = jax.nn.sigmoid(proj[3]) * proj[2]
    triangle_product = jnp.einsum('hik,hjk->hij', left, right, precision=hp)
    hidden_state = channel_norm(triangle_product, output_gain)
    mixed = jnp.einsum('hc,hij->cij', w_out, hidden_state, precision=hp)
    gate = jax.nn.sigmoid(jnp.einsum('dc,dij->cij', w_gate, normed, precision=hp))
    return gate * mixed

def reference(pair, in_gain, output_gain, w_edges, w_gate, w_out, cotangent):
    update, pullback = jax.vjp(forward, pair, in_gain, output_gain, w_edges, w_gate, w_out)
    d_pair, d_in_gain, d_out_gain, d_edges, d_gate, d_out = pullback(cotangent)
    return (update, d_pair, d_in_gain, d_out_gain, d_edges, d_gate, d_out)
```

```python
import functools

import jax
import jax.numpy as jnp
from jax import lax
from jax.experimental import pallas as pl
from jax.experimental.pallas import tpu as pltpu
from jax.sharding import PartitionSpec as P

HIDDEN_WIDTH = 128
EPS = 1e-05
F32 = jnp.float32
BF16 = jnp.bfloat16
LANES = 128


def spread(pair, in_gain, output_gain, w_edges, w_gate, w_out, cotangent):
    hp = lax.Precision.HIGHEST
    shard_c = pair.shape[0]
    whole = lax.all_gather(pair, "chan", axis=0, tiled=True)
    centred = whole - jnp.mean(whole, 0)
    pair_rstd = lax.rsqrt(jnp.mean(centred * centred, 0) + 1e-05)
    zhat = centred * pair_rstd
    normed = zhat * in_gain[:, None, None]
    proj = jnp.einsum("ech,crn->ehrn", w_edges, normed, precision=hp)
    left_sig = jax.nn.sigmoid(proj[1])
    left = left_sig * proj[0]
    right_sig = jax.nn.sigmoid(proj[3])
    right = right_sig * proj[2]
    gate = jax.nn.sigmoid(jnp.einsum("dc,drn->crn", w_gate, normed, precision=hp))
    right_all = lax.all_gather(right, "row", axis=1, tiled=True)
    triangle_product = jnp.einsum("hrk,hjk->hrj", left, right_all, precision=hp)
    first, second = lax.psum(
        (jnp.sum(triangle_product, 0), jnp.sum(triangle_product * triangle_product, 0)), "chan"
    )
    hidden_average = first / HIDDEN_WIDTH
    hidden_inverse_deviation = lax.rsqrt(
        second / HIDDEN_WIDTH - hidden_average * hidden_average + 1e-05
    )
    normalized_hidden = (triangle_product - hidden_average) * hidden_inverse_deviation
    hidden_state = normalized_hidden * output_gain[:, None, None]
    mixed = lax.psum_scatter(
        jnp.einsum("hc,hrn->crn", w_out, hidden_state, precision=hp),
        "chan",
        scatter_dimension=0,
        tiled=True,
    )
    update = gate * mixed
    d_mixed = cotangent * gate
    d_gate_pre = cotangent * mixed * gate * (1.0 - gate)
    d_mixed_all = lax.all_gather(d_mixed, "chan", axis=0, tiled=True)
    hidden_gradient = jnp.einsum("hc,crn->hrn", w_out, d_mixed_all, precision=hp)
    g_out = jnp.einsum("hrn,crn->hc", hidden_state, d_mixed_all, precision=hp)
    output_gain_gradient = jnp.sum(normalized_hidden * hidden_gradient, (1, 2))
    normalized_gradient = hidden_gradient * output_gain[:, None, None]
    first_average_term, second_average_term = lax.psum(
        (jnp.sum(normalized_gradient, 0), jnp.sum(normalized_gradient * normalized_hidden, 0)),
        "chan",
    )
    triangle_gradient = hidden_inverse_deviation * (
        normalized_gradient
        - first_average_term / HIDDEN_WIDTH
        - normalized_hidden * (second_average_term / HIDDEN_WIDTH)
    )
    d_tri_cols = lax.all_to_all(triangle_gradient, "row", split_axis=2, concat_axis=1, tiled=True)
    d_left = jnp.einsum("hrj,hjk->hrk", triangle_gradient, right_all, precision=hp)
    d_right = jnp.einsum(
        "hij,hik->hjk", d_tri_cols, lax.all_gather(left, "row", axis=1, tiled=True), precision=hp
    )
    d_proj = jnp.stack(
        [
            d_left * left_sig,
            d_left * proj[0] * left_sig * (1.0 - left_sig),
            d_right * right_sig,
            d_right * proj[2] * right_sig * (1.0 - right_sig),
        ]
    )
    g_edges = jnp.einsum("crn,ehrn->ech", normed, d_proj, precision=hp)
    g_gate = jnp.einsum("drn,crn->dc", normed, d_gate_pre, precision=hp)
    offset = lax.axis_index("chan") * shard_c
    first_part = jnp.einsum("ech,ehrn->crn", w_edges, d_proj, precision=hp)
    d_normed = lax.psum(
        first_part + jnp.einsum("dc,crn->drn", w_gate, d_gate_pre, precision=hp), "chan"
    )
    d_zhat = d_normed * in_gain[:, None, None]
    first_mean = jnp.mean(d_zhat, 0)
    second_mean = jnp.mean(d_zhat * zhat, 0)
    d_full = pair_rstd * (d_zhat - first_mean - zhat * second_mean)
    d_pair = lax.dynamic_slice_in_dim(d_full, offset, shard_c, 0)
    g_in_gain = lax.dynamic_slice_in_dim(jnp.sum(zhat * d_normed, (1, 2)), offset, shard_c, 0)
    totals = lax.psum((g_in_gain, output_gain_gradient, g_edges, g_gate, g_out), "row")
    return (update, d_pair, totals[0], totals[1], totals[2], totals[3], totals[4])


def split(x):
    hi = x.astype(BF16)
    return hi, (x - hi.astype(F32)).astype(BF16)


def dot3(a, b, dims=((1,), (0,))):
    (ah, al), (bh, bl) = a, b
    dot = functools.partial(lax.dot_general, dimension_numbers=(dims, ((), ())), preferred_element_type=F32)
    return dot(ah, bh) + (dot(ah, bl) + dot(al, bh))


def mean_lanes(x):
    return jnp.mean(x, axis=-1, keepdims=True)


def norm_lanes(x):
    centred = x - mean_lanes(x)
    rstd = lax.rsqrt(mean_lanes(centred * centred) + EPS)
    return centred * rstd, rstd


def prepare_kernel(gain_ref, we, wg, wo, oe, og, oo, wnh, wnl, wth, wtl, woh, wol, wqh, wql):
    s, c = wg.shape
    chan = lax.axis_index("chan")
    gain = gain_ref[...]

    def put(k, both):
        at = slice(k * c, (k + 1) * c)
        wnh[at, :], wnl[at, :] = split(both)
        wth[:, at], wtl[:, at] = split(both.T)

    for e in range(4):
        put(e, jnp.concatenate([we[e], oe[e * s : (e + 1) * s, :]], axis=0) * gain)
    own, other = wg[...] * gain, og[...] * gain
    put(4, jnp.concatenate([jnp.where(chan == 0, own, other), jnp.where(chan == 0, other, own)], axis=0))
    both = jnp.concatenate([wo[...], oo[...]], axis=0)
    woh[...], wol[...] = split(both)
    wqh[...], wql[...] = split(both.T)


def prepare(gain, w_e, w_g, w_o, other):
    s, c = w_g.shape
    vm = pl.BlockSpec(memory_space=pltpu.VMEM)
    shapes = [(5 * c, c)] * 2 + [(c, 5 * c)] * 2 + [(c, c)] * 4
    return pl.pallas_call(
        prepare_kernel,
        out_shape=[jax.ShapeDtypeStruct(x, BF16) for x in shapes],
        in_specs=[vm] * 7,
        out_specs=[vm] * 8,
        compiler_params=pltpu.CompilerParams(vmem_limit_bytes=8 << 20),
        name="prepare",
    )(gain, w_e, w_g, w_o, *other)


def products(n, rows, x_row, y_ref):
    acc = [jnp.zeros((n // 8, 8, LANES), F32) for _ in range(rows)]
    for m in range(n):
        y = y_ref[m * n : (m + 1) * n, :].reshape(n // 8, 8, LANES)
        for a in range(rows):
            acc[a] = acc[a] + x_row(a, m)[None] * y
    return jnp.concatenate([part.reshape(n, LANES) for part in acc], axis=0)


def update_kernel(
    n, x_ref, y_ref, gain_ref, out_gain_ref, we, wg, oe, og, wnh, wnl, wth, wtl, woh, wol, wqh, wql,
    up_ref, dp_ref, dig_ref, dog_ref, de_ref, dg_ref, do_ref,
    ct, zh, zl, left, s1, right, s3, right_t, gate, upd, xh, xl, mh, ml, dtri, dgp, dh, dl, zown, rown, grads,
):
    c, s = LANES, LANES // 2
    blk = up_ref.shape[0]
    q = blk // n
    upper = x_ref.shape[0] // (4 * blk)
    row, chan = lax.axis_index("row"), lax.axis_index("chan")
    zy, core = row // 2, row % 2
    rows = 4
    cells = rows * n
    low = lax.broadcasted_iota(jnp.int32, (blk, c), 1) < s

    def project(t, carry):
        zpos, ypos = t % upper, t // upper
        base = (zpos + upper * 2 * ypos) * blk
        first_at = pl.multiple_of(base + upper * blk * chan, blk)
        second_at = pl.multiple_of(base + upper * blk * (1 - chan), blk)
        target = zy ^ (zpos * 2 + ypos)
        pair, places = [], []
        for k, ref in enumerate((x_ref, y_ref)):
            first, second = ref[pl.ds(first_at, blk), :], ref[pl.ds(second_at, blk), :]
            pair.append(jnp.where(low, first, pltpu.roll(second, s, 1)))
            at = pl.multiple_of((target * 2 + (core ^ k)) * blk, blk)
            places.append(at)
            ct[pl.ds(at, blk), :] = jnp.where(low, pltpu.roll(first, s, 1), second)
        zhat, rstd = norm_lanes(jnp.concatenate(pair, axis=0))
        z = split(zhat)

        @pl.when(t == 0)
        def _():
            zown[...] = zhat[:blk]
            rown[...] = jnp.broadcast_to(rstd[:blk], (blk, c))

        proj = dot3(z, (wth[...], wtl[...]))
        sl = jax.nn.sigmoid(proj[:, c : 2 * c])
        le = sl * proj[:, :c]
        sr = jax.nn.sigmoid(proj[:, 3 * c : 4 * c])
        ri = sr * proj[:, 2 * c : 3 * c]
        ga = jax.nn.sigmoid(proj[:, 4 * c :])
        for k in range(2):
            here, part = pl.ds(places[k], blk), slice(k * blk, (k + 1) * blk)
            zh[here, :], zl[here, :] = z[0][part], z[1][part]
            left[here, :], s1[here, :] = le[part], sl[part]
            right[here, :], s3[here, :] = ri[part], sr[part]
            gate[here, :] = ga[part]
            for r in range(q):
                at = k * blk + r * n
                right_t[pl.ds(places[k] // n + r, n, stride=n), :] = ri[at : at + n]
        return carry

    lax.fori_loop(0, 2 * upper, project, 0)

    def row_of(ref, at):
        return ref[pl.ds(at, 8, stride=0), :]

    def triangle(b, total):
        r0 = pl.multiple_of(b * cells, cells)
        here = pl.ds(r0, cells)
        tri = products(n, rows, lambda a, m: row_of(left, r0 + a * n + m), right_t)
        xhat, rstd = norm_lanes(tri)
        x = split(xhat * out_gain_ref[...])
        xh[here, :], xl[here, :] = x
        mixed = dot3(x, (woh[...], wol[...]))
        ga = gate[here, :]
        upd[here, :] = ga * mixed
        dm = ct[here, :] * ga
        m = split(dm)
        mh[here, :], ml[here, :] = m
        dgp[here, :] = dm * mixed * (1.0 - ga)
        hidden = dot3(m, (wqh[...], wql[...]))
        ng = hidden * out_gain_ref[...]
        dtri[here, :] = rstd * (ng - mean_lanes(ng) - xhat * mean_lanes(ng * xhat))
        return total + jnp.sum(xhat * hidden, axis=0, keepdims=True)

    total = lax.fori_loop(0, n // rows, triangle, jnp.zeros((1, c), F32))
    dog_ref[...] = total[:, :s]

    def gradients(b, carry):
        r0 = pl.multiple_of(b * cells, cells)
        here = pl.ds(r0, cells)
        dle = products(n, rows, lambda a, m: row_of(dtri, r0 + a * n + m), right)
        a = s1[here, :]
        dh[here, :c], dl[here, :c] = split(dle * a)
        dh[here, c : 2 * c], dl[here, c : 2 * c] = split(dle * left[here, :] * (1.0 - a))
        dri = products(n, rows, lambda a, m: row_of(dtri, m * n + b * rows + a), left)
        a = s3[here, :]
        dh[here, 2 * c : 3 * c], dl[here, 2 * c : 3 * c] = split(dri * a)
        dh[here, 3 * c : 4 * c], dl[here, 3 * c : 4 * c] = split(dri * right[here, :] * (1.0 - a))
        dh[here, 4 * c :], dl[here, 4 * c :] = split(dgp[here, :])
        return carry

    lax.fori_loop(0, n // rows, gradients, 0)

    down = ((0,), (0,))
    grads[...] = dot3((dh[...], dl[...]), (zh[...], zl[...]), down)
    do_ref[...] = dot3((xh[:, :s], xl[:, :s]), (mh[...], ml[...]), down)

    gain = gain_ref[...]
    mine = pl.ds(pl.multiple_of(4 * c + s * chan, s), s)
    others = pl.ds(pl.multiple_of(4 * c + s * (1 - chan), s), s)
    dg_ref[...] = grads[mine, :] * gain
    weighted = wg[...] * grads[mine, :] + og[...] * grads[others, :]
    for e in range(4):
        mine, others = grads[e * c : e * c + s, :], grads[e * c + s : (e + 1) * c, :]
        de_ref[e] = mine * gain
        weighted = weighted + we[e] * mine + oe[e * s : (e + 1) * s, :] * others
    d_gain = jnp.sum(weighted, axis=0, keepdims=True)

    def half(x):
        return jnp.where(chan == 0, x[:, :s], pltpu.roll(x, s, 1)[:, :s])

    dig_ref[...] = half(jnp.broadcast_to(d_gain, (8, c)))[:1]
    here = pl.ds(pl.multiple_of(row * blk, blk), blk)
    up_ref[...] = half(upd[here, :])
    dz = dot3((dh[here, :], dl[here, :]), (wnh[...], wnl[...]))
    zhat = zown[...]
    dp_ref[...] = half(rown[...] * (dz - mean_lanes(dz) - zhat * mean_lanes(dz * zhat)))


def whole_update(n, blk, x, y, gain, out_gain, w_e, w_g, other, ready):
    c, s = LANES, LANES // 2
    vm = pl.BlockSpec(memory_space=pltpu.VMEM)
    cells = n * n
    out = [(blk, s), (blk, s), (1, s), (1, s), (4, s, c), (s, c), (s, c)]
    full, half = pltpu.VMEM((cells, c), F32), pltpu.VMEM((cells, c), BF16)
    scratch = (
        [full, half, half] + [full] * 7 + [half] * 4 + [full] * 2
        + [pltpu.VMEM((cells, 5 * c), BF16)] * 2 + [pltpu.VMEM((blk, c), F32)] * 2 + [pltpu.VMEM((5 * c, c), F32)]
    )
    return pl.pallas_call(
        functools.partial(update_kernel, n),
        out_shape=[jax.ShapeDtypeStruct(shape, F32) for shape in out],
        in_specs=[vm] * 16,
        out_specs=[vm] * 7,
        scratch_shapes=scratch,
        compiler_params=pltpu.CompilerParams(vmem_limit_bytes=32 << 20),
        name="whole_update",
    )(x, y, gain, out_gain, w_e, w_g, *other, *ready)


def gathered(devices, pair, in_gain, output_gain, w_edges, w_gate, w_out, cotangent):
    s, q, n = pair.shape
    c = 2 * s
    blk = q * n

    def swap(x, bits):
        return lax.ppermute(x, ("row", "chan"), [(i, i ^ bits) for i in range(devices)])

    def cells_of(x):
        return jnp.transpose(x, (1, 2, 0)).reshape(blk, s)

    w_e = jnp.transpose(w_edges, (0, 2, 1))
    w_g = jnp.transpose(w_gate)
    held = jnp.concatenate([cells_of(pair), cells_of(cotangent)], axis=1)
    mine = jnp.concatenate([w_e.reshape(4 * s, c), w_g, w_out, jnp.pad(output_gain[None], ((0, 7), (0, s)))])
    bits = 8
    while bits < devices:
        held = jnp.concatenate([held, swap(held, bits)])
        bits *= 2
    theirs = swap(mine, 1)
    held = jnp.concatenate([held, swap(held, 1), swap(held, 4), swap(held, 5)])
    beside = swap(held, 2)
    o_e, o_g, o_o = theirs[: 4 * s], theirs[4 * s : 5 * s], theirs[5 * s : 6 * s]
    gain = in_gain[None]
    out_gain = jnp.concatenate([output_gain[None], theirs[6 * s : 6 * s + 1, :s]], axis=1)
    ready = prepare(gain, w_e, w_g, w_out, (o_e, o_g, o_o))
    up, dp, dig, dog, de, dg, do = whole_update(n, blk, held, beside, gain, out_gain, w_e, w_g, (o_e, o_g), ready)

    def pair_of(x):
        return jnp.transpose(x.reshape(q, n, s), (2, 0, 1))

    return (pair_of(up), pair_of(dp), dig[0], dog[0], jnp.transpose(de, (0, 2, 1)), jnp.transpose(dg), do)


def solution(mesh):
    devices, chans = mesh.size, mesh.shape["chan"]

    def shards(pair, in_gain, output_gain, w_edges, *rest):
        n, c = pair.shape[2], w_edges.shape[1]
        fits = (
            chans == 2 and devices >= 8 and devices & (devices - 1) == 0 and n <= 32 and n % 8 == 0
            and c == LANES and w_edges.shape[2] * chans == LANES and (pair.shape[1] * n) % 16 == 0
        )
        step = functools.partial(gathered, devices) if fits else spread
        return step(pair, in_gain, output_gain, w_edges, *rest)

    placed = (
        P("chan", "row", None),
        P(),
        P("chan"),
        P(None, None, "chan"),
        P(None, "chan"),
        P("chan", None),
        P("chan", "row", None),
    )
    return jax.shard_map(
        shards,
        mesh=mesh,
        in_specs=placed,
        out_specs=(placed[0], placed[0], P("chan"), P("chan"), placed[3], placed[4], placed[5]),
        check_vma=False,
    )
```

```python
import functools

import jax
import jax.numpy as jnp
from jax import lax
from jax.experimental import pallas as pl
from jax.experimental.pallas import tpu as pltpu
from jax.sharding import PartitionSpec as P

HIDDEN_WIDTH = 128
EPS = 1e-05
F32 = jnp.float32
BF16 = jnp.bfloat16
LANES = 128
ROWS = 8


def spread(pair, in_gain, output_gain, w_edges, w_gate, w_out, cotangent):
    hp = lax.Precision.HIGHEST
    shard_c = pair.shape[0]
    whole = lax.all_gather(pair, "chan", axis=0, tiled=True)
    centred = whole - jnp.mean(whole, 0)
    pair_rstd = lax.rsqrt(jnp.mean(centred * centred, 0) + 1e-05)
    zhat = centred * pair_rstd
    normed = zhat * in_gain[:, None, None]
    proj = jnp.einsum("ech,crn->ehrn", w_edges, normed, precision=hp)
    left_sig = jax.nn.sigmoid(proj[1])
    left = left_sig * proj[0]
    right_sig = jax.nn.sigmoid(proj[3])
    right = right_sig * proj[2]
    gate = jax.nn.sigmoid(jnp.einsum("dc,drn->crn", w_gate, normed, precision=hp))
    right_all = lax.all_gather(right, "row", axis=1, tiled=True)
    triangle_product = jnp.einsum("hrk,hjk->hrj", left, right_all, precision=hp)
    first, second = lax.psum(
        (jnp.sum(triangle_product, 0), jnp.sum(triangle_product * triangle_product, 0)), "chan"
    )
    hidden_average = first / HIDDEN_WIDTH
    hidden_inverse_deviation = lax.rsqrt(
        second / HIDDEN_WIDTH - hidden_average * hidden_average + 1e-05
    )
    normalized_hidden = (triangle_product - hidden_average) * hidden_inverse_deviation
    hidden_state = normalized_hidden * output_gain[:, None, None]
    mixed = lax.psum_scatter(
        jnp.einsum("hc,hrn->crn", w_out, hidden_state, precision=hp),
        "chan",
        scatter_dimension=0,
        tiled=True,
    )
    update = gate * mixed
    d_mixed = cotangent * gate
    d_gate_pre = cotangent * mixed * gate * (1.0 - gate)
    d_mixed_all = lax.all_gather(d_mixed, "chan", axis=0, tiled=True)
    hidden_gradient = jnp.einsum("hc,crn->hrn", w_out, d_mixed_all, precision=hp)
    g_out = jnp.einsum("hrn,crn->hc", hidden_state, d_mixed_all, precision=hp)
    output_gain_gradient = jnp.sum(normalized_hidden * hidden_gradient, (1, 2))
    normalized_gradient = hidden_gradient * output_gain[:, None, None]
    first_average_term, second_average_term = lax.psum(
        (jnp.sum(normalized_gradient, 0), jnp.sum(normalized_gradient * normalized_hidden, 0)),
        "chan",
    )
    triangle_gradient = hidden_inverse_deviation * (
        normalized_gradient
        - first_average_term / HIDDEN_WIDTH
        - normalized_hidden * (second_average_term / HIDDEN_WIDTH)
    )
    d_tri_cols = lax.all_to_all(triangle_gradient, "row", split_axis=2, concat_axis=1, tiled=True)
    d_left = jnp.einsum("hrj,hjk->hrk", triangle_gradient, right_all, precision=hp)
    d_right = jnp.einsum(
        "hij,hik->hjk", d_tri_cols, lax.all_gather(left, "row", axis=1, tiled=True), precision=hp
    )
    d_proj = jnp.stack(
        [
            d_left * left_sig,
            d_left * proj[0] * left_sig * (1.0 - left_sig),
            d_right * right_sig,
            d_right * proj[2] * right_sig * (1.0 - right_sig),
        ]
    )
    g_edges = jnp.einsum("crn,ehrn->ech", normed, d_proj, precision=hp)
    g_gate = jnp.einsum("drn,crn->dc", normed, d_gate_pre, precision=hp)
    offset = lax.axis_index("chan") * shard_c
    first_part = jnp.einsum("ech,ehrn->crn", w_edges, d_proj, precision=hp)
    d_normed = lax.psum(
        first_part + jnp.einsum("dc,crn->drn", w_gate, d_gate_pre, precision=hp), "chan"
    )
    d_zhat = d_normed * in_gain[:, None, None]
    first_mean = jnp.mean(d_zhat, 0)
    second_mean = jnp.mean(d_zhat * zhat, 0)
    d_full = pair_rstd * (d_zhat - first_mean - zhat * second_mean)
    d_pair = lax.dynamic_slice_in_dim(d_full, offset, shard_c, 0)
    g_in_gain = lax.dynamic_slice_in_dim(jnp.sum(zhat * d_normed, (1, 2)), offset, shard_c, 0)
    totals = lax.psum((g_in_gain, output_gain_gradient, g_edges, g_gate, g_out), "row")
    return (update, d_pair, totals[0], totals[1], totals[2], totals[3], totals[4])


def split(x):
    hi = x.astype(BF16)
    return hi, (x - hi.astype(F32)).astype(BF16)


def dot(a, b):
    return jnp.dot(a, b, preferred_element_type=F32)


def mean_lanes(x):
    return jnp.mean(x, axis=-1, keepdims=True)


def norm_lanes(x):
    centred = x - mean_lanes(x)
    rstd = lax.rsqrt(mean_lanes(centred * centred) + EPS)
    return centred * rstd, rstd


def prepare_kernel(gain_ref, we, wg, wo, oe, og, oo, wnh, wnl, wdh, wtl, woh, wol, wqh, wql):
    s, c = wg.shape
    chan = lax.axis_index("chan")
    gain = gain_ref[...]

    def put(k, both):
        at = slice(k * c, (k + 1) * c)
        wnh[at, :], wnl[at, :] = split(both)
        high, wtl[:, at] = split(both.T)
        wdh[:c, at] = high
        wdh[c:, at] = high

    for e in range(4):
        put(e, jnp.concatenate([we[e], oe[e * s : (e + 1) * s, :]], axis=0) * gain)
    own, other = wg[...] * gain, og[...] * gain
    put(4, jnp.concatenate([jnp.where(chan == 0, own, other), jnp.where(chan == 0, other, own)], axis=0))
    both = jnp.concatenate([wo[...], oo[...]], axis=0)
    high, wol[...] = split(both)
    woh[:c, :] = high
    woh[c:, :] = high
    high, wql[...] = split(both.T)
    wqh[:c, :] = high
    wqh[c:, :] = high


def prepare(gain, w_e, w_g, w_o, other):
    s, c = w_g.shape
    vm = pl.BlockSpec(memory_space=pltpu.VMEM)
    shapes = [(5 * c, c), (5 * c, c), (2 * c, 5 * c), (c, 5 * c), (2 * c, c), (c, c), (2 * c, c), (c, c)]
    return pl.pallas_call(
        prepare_kernel,
        out_shape=[jax.ShapeDtypeStruct(x, BF16) for x in shapes],
        in_specs=[vm] * 7,
        out_specs=[vm] * 8,
        compiler_params=pltpu.CompilerParams(vmem_limit_bytes=8 << 20),
        name="prepare",
    )(gain, w_e, w_g, w_o, *other)


def products(n, rows, x_row, y_ref):
    acc = [jnp.zeros((n // 8, 8, LANES), F32) for _ in range(rows)]
    for m in range(n):
        y = y_ref[m * n : (m + 1) * n, :].reshape(n // 8, 8, LANES)
        for a in range(rows):
            acc[a] = acc[a] + x_row(a, m)[None] * y
    return jnp.concatenate([part.reshape(n, LANES) for part in acc], axis=0)


def update_kernel(
    n, x_ref, y_ref, gain_ref, out_gain_ref, we, wg, oe, og, wnh, wnl, wdh, wtl, woh, wol, wqh, wql,
    up_ref, dp_ref, dig_ref, dog_ref, de_ref, dg_ref, do_ref,
    ct, z, proj, left, s1, right, s3, right_t, gate, upd, xhat, xs, rstds, ms, mid, dtri, dgp, dh, dl, zown, rown,
    grads,
):
    c, s = LANES, LANES // 2
    blk = up_ref.shape[0]
    q = blk // n
    upper = x_ref.shape[0] // (4 * blk)
    row, chan = lax.axis_index("row"), lax.axis_index("chan")
    zy, core = row // 2, row % 2
    low = lax.broadcasted_iota(jnp.int32, (blk, c), 1) < s

    def place(t, k):
        target = zy ^ (t % upper * 2 + t // upper)
        return pl.multiple_of((target * 2 + (core ^ k)) * blk, blk)

    for t in range(2 * upper):
        base = (t % upper + upper * 2 * (t // upper)) * blk
        first_at = pl.multiple_of(base + upper * blk * chan, blk)
        second_at = pl.multiple_of(base + upper * blk * (1 - chan), blk)
        pair = []
        for k, ref in enumerate((x_ref, y_ref)):
            first, second = ref[pl.ds(first_at, blk), :], ref[pl.ds(second_at, blk), :]
            pair.append(jnp.where(low, first, pltpu.roll(second, s, 1)))
            ct[pl.ds(place(t, k), blk), :] = jnp.where(low, pltpu.roll(first, s, 1), second)
        zhat, rstd = norm_lanes(jnp.concatenate(pair, axis=0))
        hi, lo = split(zhat)
        for k in range(2):
            here, part = pl.ds(place(t, k), blk), slice(k * blk, (k + 1) * blk)
            z[here, :c], z[here, c:] = hi[part], lo[part]
        if t == 0:
            zown[...] = zhat[:blk]
            rown[...] = jnp.broadcast_to(rstd[:blk], (blk, c))

    def matmul(a, high, low):
        return dot(a[...], high[...]) + dot(a[:, :c], low[...])

    proj[...] = matmul(z, wdh, wtl)
    a = jax.nn.sigmoid(proj[:, c : 2 * c])
    left[...], s1[...] = a * proj[:, :c], a
    a = jax.nn.sigmoid(proj[:, 3 * c : 4 * c])
    found = a * proj[:, 2 * c : 3 * c]
    right[...], s3[...] = found, a
    for r in range(n):
        right_t[pl.ds(r, n, stride=n), :] = found[r * n : (r + 1) * n]
    gate[...] = jax.nn.sigmoid(proj[:, 4 * c :])

    def row_of(ref, at):
        return ref[pl.ds(at, 8, stride=0), :]

    rows = ROWS
    cells = rows * n

    def triangle(b, carry):
        r0 = pl.multiple_of(b * cells, cells)
        mid[pl.ds(r0, cells), :] = products(n, rows, lambda a, m: row_of(left, r0 + a * n + m), right_t)
        return carry

    lax.fori_loop(0, n // rows, triangle, 0)
    found, rstd = norm_lanes(mid[...])
    xhat[...] = found
    rstds[...] = jnp.broadcast_to(rstd, found.shape)
    xs[:, :c], xs[:, c:] = split(found * out_gain_ref[...])
    mixed, a = matmul(xs, woh, wol), gate[...]
    upd[...] = a * mixed
    dm = ct[...] * a
    ms[:, :c], ms[:, c:] = split(dm)
    dh[:, 4 * c :], dl[:, 4 * c :] = split(dm * mixed * (1.0 - a))
    hidden, found = matmul(ms, wqh, wql), xhat[...]
    ng = hidden * out_gain_ref[...]
    dtri[...] = rstds[...] * (ng - mean_lanes(ng) - found * mean_lanes(ng * found))
    dog_ref[...] = jnp.sum(found * hidden, axis=0, keepdims=True)[:, :s]

    def left_gradient(b, carry):
        r0 = pl.multiple_of(b * cells, cells)
        mid[pl.ds(r0, cells), :] = products(n, rows, lambda a, m: row_of(dtri, r0 + a * n + m), right)
        return carry

    def right_gradient(b, carry):
        r0 = pl.multiple_of(b * cells, cells)
        xhat[pl.ds(r0, cells), :] = products(n, rows, lambda a, m: row_of(dtri, m * n + b * rows + a), left)
        return carry

    lax.fori_loop(0, n // rows, left_gradient, 0)
    lax.fori_loop(0, n // rows, right_gradient, 0)
    dle, a = mid[...], s1[...]
    dh[:, :c], dl[:, :c] = split(dle * a)
    dh[:, c : 2 * c], dl[:, c : 2 * c] = split(dle * left[...] * (1.0 - a))
    dri, a = xhat[...], s3[...]
    dh[:, 2 * c : 3 * c], dl[:, 2 * c : 3 * c] = split(dri * a)
    dh[:, 3 * c : 4 * c], dl[:, 3 * c : 4 * c] = split(dri * right[...] * (1.0 - a))

    def down(a, b):
        return lax.dot_general(a, b, (((0,), (0,)), ((), ())), preferred_element_type=F32)

    wide = down(dh[...], z[...])
    grads[...] = wide[:, :c] + (wide[:, c:] + down(dl[...], z[:, :c]))
    wide = down(xs[:, :s], ms[...])
    do_ref[...] = wide[:, :c] + (wide[:, c:] + down(xs[:, c : c + s], ms[:, :c]))

    gain = gain_ref[...]
    mine = pl.ds(pl.multiple_of(4 * c + s * chan, s), s)
    others = pl.ds(pl.multiple_of(4 * c + s * (1 - chan), s), s)
    dg_ref[...] = grads[mine, :] * gain
    weighted = wg[...] * grads[mine, :] + og[...] * grads[others, :]
    for e in range(4):
        mine, others = grads[e * c : e * c + s, :], grads[e * c + s : (e + 1) * c, :]
        de_ref[e] = mine * gain
        weighted = weighted + we[e] * mine + oe[e * s : (e + 1) * s, :] * others
    d_gain = jnp.sum(weighted, axis=0, keepdims=True)

    def half(x):
        return jnp.where(chan == 0, x[:, :s], pltpu.roll(x, s, 1)[:, :s])

    dig_ref[...] = half(jnp.broadcast_to(d_gain, (8, c)))[:1]
    here = pl.ds(pl.multiple_of(row * blk, blk), blk)
    up_ref[...] = half(upd[here, :])
    dz = dot(dh[here, :], wnh[...]) + (dot(dh[here, :], wnl[...]) + dot(dl[here, :], wnh[...]))
    zhat = zown[...]
    dp_ref[...] = half(rown[...] * (dz - mean_lanes(dz) - zhat * mean_lanes(dz * zhat)))


def whole_update(n, blk, x, y, gain, out_gain, w_e, w_g, other, ready):
    c, s = LANES, LANES // 2
    vm = pl.BlockSpec(memory_space=pltpu.VMEM)
    cells = n * n
    out = [(blk, s), (blk, s), (1, s), (1, s), (4, s, c), (s, c), (s, c)]

    def vmem(rows, width, dtype=F32):
        return pltpu.VMEM((rows, width), dtype)

    full, both = vmem(cells, c), vmem(cells, 2 * c, BF16)
    scratch = (
        [full, both, vmem(cells, 5 * c)] + [full] * 8 + [both, full, both] + [full] * 3
        + [vmem(cells, 5 * c, BF16)] * 2 + [vmem(blk, c)] * 2 + [vmem(5 * c, c)]
    )
    return pl.pallas_call(
        functools.partial(update_kernel, n),
        out_shape=[jax.ShapeDtypeStruct(shape, F32) for shape in out],
        in_specs=[vm] * 16,
        out_specs=[vm] * 7,
        scratch_shapes=scratch,
        compiler_params=pltpu.CompilerParams(vmem_limit_bytes=32 << 20),
        name="whole_update",
    )(x, y, gain, out_gain, w_e, w_g, *other, *ready)


def gathered(devices, pair, in_gain, output_gain, w_edges, w_gate, w_out, cotangent):
    s, q, n = pair.shape
    c = 2 * s
    blk = q * n

    def swap(x, bits):
        return lax.ppermute(x, ("row", "chan"), [(i, i ^ bits) for i in range(devices)])

    def cells_of(x):
        return jnp.transpose(x, (1, 2, 0)).reshape(blk, s)

    w_e = jnp.transpose(w_edges, (0, 2, 1))
    w_g = jnp.transpose(w_gate)
    held = jnp.concatenate([cells_of(pair), cells_of(cotangent)], axis=1)
    mine = jnp.concatenate([w_e.reshape(4 * s, c), w_g, w_out, jnp.pad(output_gain[None], ((0, 7), (0, s)))])
    bits = 8
    while bits < devices:
        held = jnp.concatenate([held, swap(held, bits)])
        bits *= 2
    theirs = swap(mine, 1)
    held = jnp.concatenate([held, swap(held, 1), swap(held, 4), swap(held, 5)])
    beside = swap(held, 2)
    o_e, o_g, o_o = theirs[: 4 * s], theirs[4 * s : 5 * s], theirs[5 * s : 6 * s]
    gain = in_gain[None]
    out_gain = jnp.concatenate([output_gain[None], theirs[6 * s : 6 * s + 1, :s]], axis=1)
    ready = prepare(gain, w_e, w_g, w_out, (o_e, o_g, o_o))
    up, dp, dig, dog, de, dg, do = whole_update(n, blk, held, beside, gain, out_gain, w_e, w_g, (o_e, o_g), ready)

    def pair_of(x):
        return jnp.transpose(x.reshape(q, n, s), (2, 0, 1))

    return (pair_of(up), pair_of(dp), dig[0], dog[0], jnp.transpose(de, (0, 2, 1)), jnp.transpose(dg), do)


def solution(mesh):
    devices, chans = mesh.size, mesh.shape["chan"]

    def shards(pair, in_gain, output_gain, w_edges, *rest):
        n, c = pair.shape[2], w_edges.shape[1]
        fits = (
            chans == 2 and devices >= 8 and devices & (devices - 1) == 0 and n <= 32 and n % 8 == 0
            and c == LANES and w_edges.shape[2] * chans == LANES and (pair.shape[1] * n) % 16 == 0
        )
        step = functools.partial(gathered, devices) if fits else spread
        return step(pair, in_gain, output_gain, w_edges, *rest)

    placed = (
        P("chan", "row", None),
        P(),
        P("chan"),
        P(None, None, "chan"),
        P(None, "chan"),
        P("chan", None),
        P("chan", "row", None),
    )
    return jax.shard_map(
        shards,
        mesh=mesh,
        in_specs=placed,
        out_specs=(placed[0], placed[0], P("chan"), P("chan"), placed[3], placed[4], placed[5]),
        check_vma=False,
    )
```

```python
import functools

import jax
import jax.numpy as jnp
from jax import lax
from jax.experimental import pallas as pl
from jax.experimental.pallas import tpu as pltpu
from jax.sharding import PartitionSpec as P

HIDDEN_WIDTH = 128
EPS = 1e-05
F32 = jnp.float32
BF16 = jnp.bfloat16
LANES = 128
ROWS = 8
CHUNK = 64
DEEP = 256


def spread(pair, in_gain, output_gain, w_edges, w_gate, w_out, cotangent):
    hp = lax.Precision.HIGHEST
    shard_c = pair.shape[0]
    whole = lax.all_gather(pair, "chan", axis=0, tiled=True)
    centred = whole - jnp.mean(whole, 0)
    pair_rstd = lax.rsqrt(jnp.mean(centred * centred, 0) + 1e-05)
    zhat = centred * pair_rstd
    normed = zhat * in_gain[:, None, None]
    proj = jnp.einsum("ech,crn->ehrn", w_edges, normed, precision=hp)
    left_sig = jax.nn.sigmoid(proj[1])
    left = left_sig * proj[0]
    right_sig = jax.nn.sigmoid(proj[3])
    right = right_sig * proj[2]
    gate = jax.nn.sigmoid(jnp.einsum("dc,drn->crn", w_gate, normed, precision=hp))
    right_all = lax.all_gather(right, "row", axis=1, tiled=True)
    triangle_product = jnp.einsum("hrk,hjk->hrj", left, right_all, precision=hp)
    first, second = lax.psum(
        (jnp.sum(triangle_product, 0), jnp.sum(triangle_product * triangle_product, 0)), "chan"
    )
    hidden_average = first / HIDDEN_WIDTH
    hidden_inverse_deviation = lax.rsqrt(
        second / HIDDEN_WIDTH - hidden_average * hidden_average + 1e-05
    )
    normalized_hidden = (triangle_product - hidden_average) * hidden_inverse_deviation
    hidden_state = normalized_hidden * output_gain[:, None, None]
    mixed = lax.psum_scatter(
        jnp.einsum("hc,hrn->crn", w_out, hidden_state, precision=hp),
        "chan",
        scatter_dimension=0,
        tiled=True,
    )
    update = gate * mixed
    d_mixed = cotangent * gate
    d_gate_pre = cotangent * mixed * gate * (1.0 - gate)
    d_mixed_all = lax.all_gather(d_mixed, "chan", axis=0, tiled=True)
    hidden_gradient = jnp.einsum("hc,crn->hrn", w_out, d_mixed_all, precision=hp)
    g_out = jnp.einsum("hrn,crn->hc", hidden_state, d_mixed_all, precision=hp)
    output_gain_gradient = jnp.sum(normalized_hidden * hidden_gradient, (1, 2))
    normalized_gradient = hidden_gradient * output_gain[:, None, None]
    first_average_term, second_average_term = lax.psum(
        (jnp.sum(normalized_gradient, 0), jnp.sum(normalized_gradient * normalized_hidden, 0)),
        "chan",
    )
    triangle_gradient = hidden_inverse_deviation * (
        normalized_gradient
        - first_average_term / HIDDEN_WIDTH
        - normalized_hidden * (second_average_term / HIDDEN_WIDTH)
    )
    d_tri_cols = lax.all_to_all(triangle_gradient, "row", split_axis=2, concat_axis=1, tiled=True)
    d_left = jnp.einsum("hrj,hjk->hrk", triangle_gradient, right_all, precision=hp)
    d_right = jnp.einsum(
        "hij,hik->hjk", d_tri_cols, lax.all_gather(left, "row", axis=1, tiled=True), precision=hp
    )
    d_proj = jnp.stack(
        [
            d_left * left_sig,
            d_left * proj[0] * left_sig * (1.0 - left_sig),
            d_right * right_sig,
            d_right * proj[2] * right_sig * (1.0 - right_sig),
        ]
    )
    g_edges = jnp.einsum("crn,ehrn->ech", normed, d_proj, precision=hp)
    g_gate = jnp.einsum("drn,crn->dc", normed, d_gate_pre, precision=hp)
    offset = lax.axis_index("chan") * shard_c
    first_part = jnp.einsum("ech,ehrn->crn", w_edges, d_proj, precision=hp)
    d_normed = lax.psum(
        first_part + jnp.einsum("dc,crn->drn", w_gate, d_gate_pre, precision=hp), "chan"
    )
    d_zhat = d_normed * in_gain[:, None, None]
    first_mean = jnp.mean(d_zhat, 0)
    second_mean = jnp.mean(d_zhat * zhat, 0)
    d_full = pair_rstd * (d_zhat - first_mean - zhat * second_mean)
    d_pair = lax.dynamic_slice_in_dim(d_full, offset, shard_c, 0)
    g_in_gain = lax.dynamic_slice_in_dim(jnp.sum(zhat * d_normed, (1, 2)), offset, shard_c, 0)
    totals = lax.psum((g_in_gain, output_gain_gradient, g_edges, g_gate, g_out), "row")
    return (update, d_pair, totals[0], totals[1], totals[2], totals[3], totals[4])


def split(x):
    hi = x.astype(BF16)
    return hi, (x - hi.astype(F32)).astype(BF16)


def dot(a, b):
    return jnp.dot(a, b, preferred_element_type=F32)


def matmul(a, twice_high, low):
    return dot(a, twice_high) + dot(a[:, :LANES], low)


def down(a, b):
    return lax.dot_general(a, b, (((0,), (0,)), ((), ())), preferred_element_type=F32)


def chunks(cells, step=CHUNK):
    return [slice(at, at + step) for at in range(0, cells, step)]


def mean_lanes(x):
    return jnp.mean(x, axis=-1, keepdims=True)


def norm_lanes(x):
    centred = x - mean_lanes(x)
    rstd = lax.rsqrt(mean_lanes(centred * centred) + EPS)
    return centred * rstd, rstd


def cells_from(ref, blk, upper, chan):
    half = blk // 2
    low = lax.broadcasted_iota(jnp.int32, (half, LANES), 1) < LANES // 2
    for t in range(2 * upper):
        own, other = ((0, 3), (2, 1))[t // upper]

        def block(side):
            at = (t % upper + upper * (own + (other - own) * side)) * half
            return ref[pl.ds(pl.multiple_of(at, half), half), :]

        first, second = block(chan), block(1 - chan)
        yield jnp.where(low, first, pltpu.roll(second, LANES // 2, 1))
        yield jnp.where(low, pltpu.roll(first, LANES // 2, 1), second)


def true_row(p, q, upper, rows):
    row = lax.axis_index("row")
    far, t = p // (rows // 2), p % (rows // 2) // q
    return (((row // 2) ^ (t % upper * 2 + t // upper)) * 2 + ((row % 2) ^ far)) * q + p % q


def held_row(j, q, upper, rows):
    row = lax.axis_index("row")
    apart = (row // 2) ^ (j // q // 2)
    t = apart % 2 * upper + apart // 2
    return ((row % 2) ^ (j // q % 2)) * (rows // 2) + t * q + j % q


def pack_kernel(we, wg, wo, gain, mine):
    s = wg.shape[0]
    for e in range(4):
        mine[e * s : (e + 1) * s, :] = we[e]
    mine[4 * s : 5 * s, :] = wg[...]
    mine[5 * s : 6 * s, :] = wo[...]
    mine[6 * s :, :] = gain[...]


def prepare_kernel(gain_ref, mine, other, wnh, wnl, wdh, wtl, woh, wol, wqh, wql, gain_out):
    c = LANES
    s = c // 2
    chan = lax.axis_index("chan")
    gain = gain_ref[...]

    def both(k):
        at = slice(k * s, (k + 1) * s)
        return mine[at, :], other[at, :]

    def put(k, whole):
        at = slice(k * c, (k + 1) * c)
        wnh[at, :], wnl[at, :] = split(whole)
        high, wtl[:, at] = split(whole.T)
        wdh[:c, at] = high
        wdh[c:, at] = high

    for e in range(4):
        put(e, jnp.concatenate(both(e), axis=0) * gain)
    a, b = both(4)
    put(4, jnp.concatenate([jnp.where(chan == 0, a, b), jnp.where(chan == 0, b, a)], axis=0) * gain)
    whole = jnp.concatenate(both(5), axis=0)
    high, wol[...] = split(whole)
    woh[:c, :] = high
    woh[c:, :] = high
    high, wql[...] = split(whole.T)
    wqh[:c, :] = high
    wqh[c:, :] = high
    gain_out[:, :s] = mine[6 * s : 6 * s + 1, :s]
    gain_out[:, s:] = other[6 * s : 6 * s + 1, :s]


def project_kernel(blk, x_ref, wdh, wtl, z, left, s1, right, s3, gate, zown, rown, proj):
    c = LANES
    upper = x_ref.shape[0] // (2 * blk)
    chan = lax.axis_index("chan")
    half = blk // 2
    for k, cells in enumerate(cells_from(x_ref, blk, upper, chan)):
        at = slice(k * half, (k + 1) * half)
        zhat, rstd = norm_lanes(cells)
        z[at, :c], z[at, c:] = split(zhat)
        if k < 2 and zown is not None:
            zown[at, :] = zhat
            rown[at, :] = jnp.broadcast_to(rstd, zhat.shape)
    for at in chunks(z.shape[0], DEEP):
        proj[at, :] = matmul(z[at, :], wdh[...], wtl[...])
    for at in chunks(z.shape[0]):
        a = jax.nn.sigmoid(proj[at, c : 2 * c])
        left[at, :], s1[at, :] = a * proj[at, :c], a
        a = jax.nn.sigmoid(proj[at, 3 * c : 4 * c])
        right[at, :], s3[at, :] = a * proj[at, 2 * c : 3 * c], a
        gate[at, :] = jax.nn.sigmoid(proj[at, 4 * c :])


def products(n, x_row, y_of):
    acc = [jnp.zeros((n // 8, 8, LANES), F32) for _ in range(ROWS)]
    for m in range(n):
        y = y_of(m).reshape(n // 8, 8, LANES)
        for a in range(ROWS):
            acc[a] = acc[a] + x_row(a, m)[None] * y
    return jnp.concatenate([part.reshape(n, LANES) for part in acc], axis=0)


def row_of(ref, at):
    return ref[pl.ds(at, 8, stride=0), :]


def over_rows(n, out, body):
    def some(b, carry):
        out[pl.ds(pl.multiple_of(b * ROWS * n, ROWS * n), ROWS * n), :] = body(b * ROWS)
        return carry

    lax.fori_loop(0, n // ROWS, some, 0)


def triangle_kernel(n, q, upper, left, right, gain_ref, woh, wol, xhat, rstds, xs, mixed, right_t, tri):
    c = LANES
    for p in range(n):
        right_t[pl.ds(true_row(p, q, upper, n), n, stride=n), :] = right[p * n : (p + 1) * n, :]

    def body(first):
        return products(
            n, lambda a, m: row_of(left, (first + a) * n + m), lambda m: right_t[m * n : (m + 1) * n, :]
        )

    over_rows(n, tri, body)
    for at in chunks(n * n):
        found, rstd = norm_lanes(tri[at, :])
        xhat[at, :] = found
        rstds[at, :] = jnp.broadcast_to(rstd, found.shape)
        xs[at, :c], xs[at, c:] = split(found * gain_ref[...])
    for at in chunks(n * n, DEEP):
        mixed[at, :] = matmul(xs[at, :], woh[...], wol[...])


def gradient_kernel(
    n, x_ref, y_ref, left, right, z_n, s1_n, s3_n, gate_n, z_f, s1_f, s3_f, gate_f, zown, rown,
    xhat, rstds, xs, mixed, gain_ref, out_gain_ref, own, other, wnh, wnl, wqh, wql,
    up_ref, dp_ref, dig_ref, dog_ref, de_ref, dg_ref, do_ref, ms, dh, dl, upd, hidden, dtri, d_left, d_right, grads,
):
    c, s = LANES, LANES // 2
    blk = up_ref.shape[0]
    q = blk // n
    upper = x_ref.shape[0] // (2 * blk)
    chan = lax.axis_index("chan")
    half = blk // 2
    part = n * n // 2
    sides = ((x_ref, gate_n), (y_ref, gate_f))

    for k, (ref, gate) in enumerate(sides):
        for b, ct in enumerate(cells_from(ref, blk, upper, chan)):
            here, there = slice(b * half, (b + 1) * half), slice(k * part + b * half, k * part + (b + 1) * half)
            a, mix = gate[here, :], mixed[there, :]
            dm = ct * a
            ms[there, :c], ms[there, c:] = split(dm)
            dh[there, 4 * c :], dl[there, 4 * c :] = split(dm * mix * (1.0 - a))
            if k == 0 and b < 2:
                upd[here, :] = a * mix
    for at in chunks(n * n, DEEP):
        hidden[at, :] = matmul(ms[at, :], wqh[...], wql[...])
    total = jnp.zeros((8, c), F32)
    for at in chunks(n * n):
        found, ng = xhat[at, :], hidden[at, :] * out_gain_ref[...]
        dtri[at, :] = rstds[at, :] * (ng - mean_lanes(ng) - found * mean_lanes(ng * found))
        total = total + jnp.sum((found * hidden[at, :]).reshape(-1, 8, c), axis=0)
    dog_ref[...] = jnp.sum(total, axis=0, keepdims=True)[:, :s]

    held = [pl.multiple_of(held_row(m, q, upper, n) * n, n) for m in range(n)]

    def of_left(first):
        return products(n, lambda a, m: row_of(dtri, (first + a) * n + m), lambda m: right[pl.ds(held[m], n), :])

    def of_right(first):
        mine = [true_row(first + a, q, upper, n) for a in range(ROWS)]
        return products(n, lambda a, m: row_of(dtri, m * n + mine[a]), lambda m: left[m * n : (m + 1) * n, :])

    over_rows(n, d_left, of_left)
    over_rows(n, d_right, of_right)
    for k, (s1, s3) in enumerate(((s1_n, s3_n), (s1_f, s3_f))):
        for here in chunks(part):
            at = slice(k * part + here.start, k * part + here.stop)
            d, a = d_left[at, :], s1[here, :]
            dh[at, :c], dl[at, :c] = split(d * a)
            dh[at, c : 2 * c], dl[at, c : 2 * c] = split(d * left[at, :] * (1.0 - a))
            d, a = d_right[at, :], s3[here, :]
            dh[at, 2 * c : 3 * c], dl[at, 2 * c : 3 * c] = split(d * a)
            dh[at, 3 * c : 4 * c], dl[at, 3 * c : 4 * c] = split(d * right[at, :] * (1.0 - a))

    def turned(at, z):
        zt = z[...].T
        wide = dot(zt, dh[at, :])
        return wide[:c] + (wide[c:] + dot(zt[:c], dl[at, :]))

    def joined(high, low, b):
        wide = down(high, b)
        return wide[:, :c] + (wide[:, c:] + down(low, b[:, :c]))

    grads[...] = (turned(slice(0, part), z_n) + turned(slice(part, 2 * part), z_f)).T
    do_ref[...] = joined(xs[:, :s], xs[:, c : c + s], ms[...])

    gain = gain_ref[...]
    mine = pl.ds(pl.multiple_of(4 * c + s * chan, s), s)
    others = pl.ds(pl.multiple_of(4 * c + s * (1 - chan), s), s)
    dg_ref[...] = grads[mine, :] * gain
    weighted = own[4 * s : 5 * s, :] * grads[mine, :] + other[4 * s : 5 * s, :] * grads[others, :]
    for e in range(4):
        mine, others = grads[e * c : e * c + s, :], grads[e * c + s : (e + 1) * c, :]
        de_ref[e] = mine * gain
        at = slice(e * s, (e + 1) * s)
        weighted = weighted + own[at, :] * mine + other[at, :] * others
    d_gain = jnp.sum(weighted, axis=0, keepdims=True)

    def own_half(x):
        return jnp.where(chan == 0, x[:, :s], pltpu.roll(x, s, 1)[:, :s])

    dig_ref[...] = own_half(jnp.broadcast_to(d_gain, (8, c)))[:1]
    up_ref[...] = own_half(upd[...])
    dz = dot(dh[:blk, :], wnh[...]) + (dot(dh[:blk, :], wnl[...]) + dot(dl[:blk, :], wnh[...]))
    zhat = zown[...]
    dp_ref[...] = own_half(rown[...] * (dz - mean_lanes(dz) - zhat * mean_lanes(dz * zhat)))


def rest_kernel(
    n, blk, x_ref, y_ref, pair_ref, z_n, left_n, s1_n, right_n, s3_n, gate_n, zown, rown, gain_ref, out_gain_ref, own,
    other, wnh, wnl, wdh, wtl, woh, wol, wqh, wql, up_ref, dp_ref, dig_ref, dog_ref, de_ref, dg_ref, do_ref,
    left, right, z_f, s1_f, s3_f, gate_f, xhat, rstds, xs, mixed, right_t, tri, proj, *scratch,
):
    q, upper, part = blk // n, x_ref.shape[0] // (2 * blk), n * n // 2
    left[:part, :], right[:part, :] = left_n[...], right_n[...]
    left_f, right_f = left.at[pl.ds(part, part)], right.at[pl.ds(part, part)]
    project_kernel(blk, pair_ref, wdh, wtl, z_f, left_f, s1_f, right_f, s3_f, gate_f, None, None, proj)
    triangle_kernel(n, q, upper, left, right, out_gain_ref, woh, wol, xhat, rstds, xs, mixed, right_t, tri)
    gradient_kernel(
        n, x_ref, y_ref, left, right, z_n, s1_n, s3_n, gate_n, z_f, s1_f, s3_f, gate_f, zown, rown,
        xhat, rstds, xs, mixed, gain_ref, out_gain_ref, own, other, wnh, wnl, wqh, wql,
        up_ref, dp_ref, dig_ref, dog_ref, de_ref, dg_ref, do_ref, *scratch,
    )


def call(kernel, name, out, scratch, limit, flops, *args):
    vm = pl.BlockSpec(memory_space=pltpu.VMEM)
    return pl.pallas_call(
        kernel,
        out_shape=[jax.ShapeDtypeStruct(shape, dtype) for shape, dtype in out],
        in_specs=[vm] * len(args),
        out_specs=[vm] * len(out),
        scratch_shapes=[pltpu.VMEM(shape, dtype) for shape, dtype in scratch],
        compiler_params=pltpu.CompilerParams(vmem_limit_bytes=limit << 20),
        cost_estimate=pl.CostEstimate(flops=flops, bytes_accessed=1 << 10, transcendentals=0),
        name=name,
    )(*args)


def gathered(devices, pair, in_gain, output_gain, w_edges, w_gate, w_out, cotangent):
    s, q, n = pair.shape
    c = 2 * s
    blk = q * n
    cells = n * n
    upper = devices // 8

    def swap(x, bits):
        return lax.ppermute(x, ("row", "chan"), [(i, i ^ bits) for i in range(devices)])

    def packed(x):
        x = jnp.transpose(x, (1, 2, 0)).reshape(2, blk // 2, s)
        return jnp.concatenate([x[0], x[1]], axis=1)[None]

    w_e = jnp.transpose(w_edges, (0, 2, 1))
    w_g = jnp.transpose(w_gate)
    held = jnp.concatenate([packed(pair), packed(cotangent)])
    gain_row = jnp.pad(output_gain[None], ((0, 7), (0, s)))
    held, gain_row = lax.optimization_barrier((held, gain_row))
    (mine,) = call(pack_kernel, "pack", [((6 * s + 8, c), F32)], [], 8, 1 << 20, w_e, w_g, w_out, gain_row)
    held = jnp.concatenate([held, swap(held, 8)], axis=1)
    other = swap(mine, 1)
    held, mine = lax.optimization_barrier((held, mine))
    bits = 16
    while bits < devices:
        held = jnp.concatenate([held, swap(held, bits)], axis=1)
        bits *= 2
    parts = [swap(held, bits) for bits in (1, 4, 5)]

    gain = in_gain[None]
    wnh, wnl, wdh, wtl, woh, wol, wqh, wql, out_gain = call(
        prepare_kernel,
        "prepare",
        [(x, BF16) for x in [(5 * c, c), (5 * c, c), (2 * c, 5 * c), (c, 5 * c), (2 * c, c), (c, c), (2 * c, c), (c, c)]]
        + [((1, c), F32)],
        [],
        8,
        1 << 20,
        gain, mine, other,
    )
    parts, wdh = lax.optimization_barrier((parts, wdh))
    held = jnp.concatenate([held, *parts[::-1]], axis=1)
    pairs, cots = held[0], held[1]
    pairs_far = swap(pairs, 2)
    cots_far = swap(cots, 2)

    full, both, wide = ((cells, c), F32), ((cells, 2 * c), BF16), ((cells, 5 * c), BF16)
    part, own = ((cells // 2, c), F32), ((blk, c), F32)
    half, many = [((cells // 2, 2 * c), BF16)] + [part] * 5, ((cells // 2, 5 * c), F32)
    near = call(
        functools.partial(project_kernel, blk), "project", half + [own] * 2, [many], 16, 1 << 30, pairs, wdh, wtl
    )
    up, dp, dig, dog, de, dg, do = call(
        functools.partial(rest_kernel, n, blk),
        "rest",
        [(x, F32) for x in [(blk, s), (blk, s), (1, s), (1, s), (4, s, c), (s, c), (s, c)]],
        [full, full] + half[:1] + [part] * 3 + [full, full, both, full, full, full, many]
        + [both, wide, wide, own] + [full] * 4 + [((5 * c, c), F32)],
        32,
        1 << 33,
        cots, cots_far, pairs_far, *near, gain, out_gain, mine, other, wnh, wnl, wdh, wtl, woh, wol, wqh, wql,
    )

    def pair_of(x):
        return jnp.transpose(x.reshape(q, n, s), (2, 0, 1))

    return (pair_of(up), pair_of(dp), dig[0], dog[0], jnp.transpose(de, (0, 2, 1)), jnp.transpose(dg), do)


def solution(mesh):
    devices, chans = mesh.size, mesh.shape["chan"]

    def shards(pair, in_gain, output_gain, w_edges, *rest):
        n, c = pair.shape[2], w_edges.shape[1]
        fits = (
            chans == 2 and devices >= 8 and devices & (devices - 1) == 0 and n <= 32 and n % 16 == 0
            and c == LANES and w_edges.shape[2] * chans == LANES and (pair.shape[1] * n) % 32 == 0
        )
        step = functools.partial(gathered, devices) if fits else spread
        return step(pair, in_gain, output_gain, w_edges, *rest)

    placed = (
        P("chan", "row", None),
        P(),
        P("chan"),
        P(None, None, "chan"),
        P(None, "chan"),
        P("chan", None),
        P("chan", "row", None),
    )
    return jax.shard_map(
        shards,
        mesh=mesh,
        in_specs=placed,
        out_specs=(placed[0], placed[0], P("chan"), P("chan"), placed[3], placed[4], placed[5]),
        check_vma=False,
    )
```

```python
import functools

import jax
import jax.numpy as jnp
from jax import lax
from jax.experimental import pallas as pl
from jax.experimental.pallas import tpu as pltpu
from jax.sharding import PartitionSpec as P

HIDDEN_WIDTH = 128
EPS = 1e-05
F32 = jnp.float32
BF16 = jnp.bfloat16
LANES = 128
ROWS = 16
CHUNK = 64
DEEP = 256


def spread(pair, in_gain, output_gain, w_edges, w_gate, w_out, cotangent):
    hp = lax.Precision.HIGHEST
    shard_c = pair.shape[0]
    whole = lax.all_gather(pair, "chan", axis=0, tiled=True)
    centred = whole - jnp.mean(whole, 0)
    pair_rstd = lax.rsqrt(jnp.mean(centred * centred, 0) + 1e-05)
    zhat = centred * pair_rstd
    normed = zhat * in_gain[:, None, None]
    proj = jnp.einsum("ech,crn->ehrn", w_edges, normed, precision=hp)
    left_sig = jax.nn.sigmoid(proj[1])
    left = left_sig * proj[0]
    right_sig = jax.nn.sigmoid(proj[3])
    right = right_sig * proj[2]
    gate = jax.nn.sigmoid(jnp.einsum("dc,drn->crn", w_gate, normed, precision=hp))
    right_all = lax.all_gather(right, "row", axis=1, tiled=True)
    triangle_product = jnp.einsum("hrk,hjk->hrj", left, right_all, precision=hp)
    first, second = lax.psum(
        (jnp.sum(triangle_product, 0), jnp.sum(triangle_product * triangle_product, 0)), "chan"
    )
    hidden_average = first / HIDDEN_WIDTH
    hidden_inverse_deviation = lax.rsqrt(
        second / HIDDEN_WIDTH - hidden_average * hidden_average + 1e-05
    )
    normalized_hidden = (triangle_product - hidden_average) * hidden_inverse_deviation
    hidden_state = normalized_hidden * output_gain[:, None, None]
    mixed = lax.psum_scatter(
        jnp.einsum("hc,hrn->crn", w_out, hidden_state, precision=hp),
        "chan",
        scatter_dimension=0,
        tiled=True,
    )
    update = gate * mixed
    d_mixed = cotangent * gate
    d_gate_pre = cotangent * mixed * gate * (1.0 - gate)
    d_mixed_all = lax.all_gather(d_mixed, "chan", axis=0, tiled=True)
    hidden_gradient = jnp.einsum("hc,crn->hrn", w_out, d_mixed_all, precision=hp)
    g_out = jnp.einsum("hrn,crn->hc", hidden_state, d_mixed_all, precision=hp)
    output_gain_gradient = jnp.sum(normalized_hidden * hidden_gradient, (1, 2))
    normalized_gradient = hidden_gradient * output_gain[:, None, None]
    first_average_term, second_average_term = lax.psum(
        (jnp.sum(normalized_gradient, 0), jnp.sum(normalized_gradient * normalized_hidden, 0)),
        "chan",
    )
    triangle_gradient = hidden_inverse_deviation * (
        normalized_gradient
        - first_average_term / HIDDEN_WIDTH
        - normalized_hidden * (second_average_term / HIDDEN_WIDTH)
    )
    d_tri_cols = lax.all_to_all(triangle_gradient, "row", split_axis=2, concat_axis=1, tiled=True)
    d_left = jnp.einsum("hrj,hjk->hrk", triangle_gradient, right_all, precision=hp)
    d_right = jnp.einsum(
        "hij,hik->hjk", d_tri_cols, lax.all_gather(left, "row", axis=1, tiled=True), precision=hp
    )
    d_proj = jnp.stack(
        [
            d_left * left_sig,
            d_left * proj[0] * left_sig * (1.0 - left_sig),
            d_right * right_sig,
            d_right * proj[2] * right_sig * (1.0 - right_sig),
        ]
    )
    g_edges = jnp.einsum("crn,ehrn->ech", normed, d_proj, precision=hp)
    g_gate = jnp.einsum("drn,crn->dc", normed, d_gate_pre, precision=hp)
    offset = lax.axis_index("chan") * shard_c
    first_part = jnp.einsum("ech,ehrn->crn", w_edges, d_proj, precision=hp)
    d_normed = lax.psum(
        first_part + jnp.einsum("dc,crn->drn", w_gate, d_gate_pre, precision=hp), "chan"
    )
    d_zhat = d_normed * in_gain[:, None, None]
    first_mean = jnp.mean(d_zhat, 0)
    second_mean = jnp.mean(d_zhat * zhat, 0)
    d_full = pair_rstd * (d_zhat - first_mean - zhat * second_mean)
    d_pair = lax.dynamic_slice_in_dim(d_full, offset, shard_c, 0)
    g_in_gain = lax.dynamic_slice_in_dim(jnp.sum(zhat * d_normed, (1, 2)), offset, shard_c, 0)
    totals = lax.psum((g_in_gain, output_gain_gradient, g_edges, g_gate, g_out), "row")
    return (update, d_pair, totals[0], totals[1], totals[2], totals[3], totals[4])


def split(x):
    hi = x.astype(BF16)
    return hi, (x - hi.astype(F32)).astype(BF16)


def dot(a, b):
    return jnp.dot(a, b, preferred_element_type=F32)


def matmul(a, twice_high, low):
    return dot(a, twice_high) + dot(a[:, :LANES], low)


def down(a, b):
    return lax.dot_general(a, b, (((0,), (0,)), ((), ())), preferred_element_type=F32)


def chunks(cells, step=CHUNK):
    return [slice(at, at + step) for at in range(0, cells, step)]


def mean_lanes(x):
    return jnp.mean(x, axis=-1, keepdims=True)


def norm_lanes(x):
    centred = x - mean_lanes(x)
    rstd = lax.rsqrt(mean_lanes(centred * centred) + EPS)
    return centred * rstd, rstd


def cells_from(ref, blk, upper, chan):
    half = blk // 2
    low = lax.broadcasted_iota(jnp.int32, (half, LANES), 1) < LANES // 2
    for t in range(2 * upper):
        own, other = ((0, 3), (2, 1))[t // upper]

        def block(side):
            at = (t % upper + upper * (own + (other - own) * side)) * half
            return ref[pl.ds(pl.multiple_of(at, half), half), :]

        first, second = block(chan), block(1 - chan)
        yield jnp.where(low, first, second)
        yield pltpu.roll(jnp.where(low, second, first), LANES // 2, 1)


def true_row(p, q, upper, rows):
    row = lax.axis_index("row")
    far, t = p // (rows // 2), p % (rows // 2) // q
    return (((row // 2) ^ (t % upper * 2 + t // upper)) * 2 + ((row % 2) ^ far)) * q + p % q


def held_row(j, q, upper, rows):
    row = lax.axis_index("row")
    apart = (row // 2) ^ (j // q // 2)
    t = apart % 2 * upper + apart // 2
    return ((row % 2) ^ (j // q % 2)) * (rows // 2) + t * q + j % q


def pack_kernel(we, wg, wo, gain, mine):
    s = wg.shape[0]
    for e in range(4):
        mine[e * s : (e + 1) * s, :] = we[e]
    mine[4 * s : 5 * s, :] = wg[...]
    mine[5 * s : 6 * s, :] = wo[...]
    mine[6 * s :, :] = gain[...]


def prepare_kernel(gain_ref, mine, other, wnh, wnl, wdh, wtl, woh, wol, wqh, wql, gain_out):
    c = LANES
    s = c // 2
    chan = lax.axis_index("chan")
    gain = gain_ref[...]

    def both(k):
        at = slice(k * s, (k + 1) * s)
        return mine[at, :], other[at, :]

    def put(k, whole):
        at = slice(k * c, (k + 1) * c)
        wnh[at, :], wnl[at, :] = split(whole)
        high, wtl[:, at] = split(whole.T)
        wdh[:c, at] = high
        wdh[c:, at] = high

    for e in range(4):
        put(e, jnp.concatenate(both(e), axis=0) * gain)
    a, b = both(4)
    put(4, jnp.concatenate([jnp.where(chan == 0, a, b), jnp.where(chan == 0, b, a)], axis=0) * gain)
    whole = jnp.concatenate(both(5), axis=0)
    high, wol[...] = split(whole)
    woh[:c, :] = high
    woh[c:, :] = high
    high, wql[...] = split(whole.T)
    wqh[:c, :] = high
    wqh[c:, :] = high
    gain_out[:, :s] = mine[6 * s : 6 * s + 1, :s]
    gain_out[:, s:] = other[6 * s : 6 * s + 1, :s]


def project_kernel(blk, x_ref, wdh, wtl, z, left, s1, right, s3, gate, zown, rown, proj):
    c = LANES
    upper = x_ref.shape[0] // (2 * blk)
    chan = lax.axis_index("chan")
    half = blk // 2
    for k, cells in enumerate(cells_from(x_ref, blk, upper, chan)):
        at = slice(k * half, (k + 1) * half)
        zhat, rstd = norm_lanes(cells)
        z[at, :c], z[at, c:] = split(zhat)
        if k < 2 and zown is not None:
            zown[at, :] = zhat
            rown[at, :] = jnp.broadcast_to(rstd, zhat.shape)
    for at in chunks(z.shape[0], DEEP):
        proj[at, :] = matmul(z[at, :], wdh[...], wtl[...])
    for at in chunks(z.shape[0]):
        a = jax.nn.sigmoid(proj[at, c : 2 * c])
        left[at, :], s1[at, :] = a * proj[at, :c], a
        a = jax.nn.sigmoid(proj[at, 3 * c : 4 * c])
        right[at, :], s3[at, :] = a * proj[at, 2 * c : 3 * c], a
        gate[at, :] = jax.nn.sigmoid(proj[at, 4 * c :])


def products(n, x_row, y_of):
    acc = [jnp.zeros((n // 8, 8, LANES), F32) for _ in range(ROWS)]
    for m in range(n):
        y = y_of(m).reshape(n // 8, 8, LANES)
        for a in range(ROWS):
            acc[a] = acc[a] + x_row(a, m)[None] * y
    return jnp.concatenate([part.reshape(n, LANES) for part in acc], axis=0)


def row_of(ref, at):
    return ref[pl.ds(at, 8, stride=0), :]


def over_rows(n, out, body):
    def some(b, carry):
        out[pl.ds(pl.multiple_of(b * ROWS * n, ROWS * n), ROWS * n), :] = body(b * ROWS)
        return carry

    lax.fori_loop(0, n // ROWS, some, 0)


def triangle_kernel(n, q, upper, left, right, gain_ref, woh, wol, xhat, rstds, xs, mixed, right_t, tri):
    c = LANES
    for p in range(n):
        right_t[pl.ds(true_row(p, q, upper, n), n, stride=n), :] = right[p * n : (p + 1) * n, :]

    def body(first):
        return products(
            n, lambda a, m: row_of(left, (first + a) * n + m), lambda m: right_t[m * n : (m + 1) * n, :]
        )

    over_rows(n, tri, body)
    for at in chunks(n * n):
        found, rstd = norm_lanes(tri[at, :])
        xhat[at, :] = found
        rstds[at, :] = jnp.broadcast_to(rstd, found.shape)
        xs[at, :c], xs[at, c:] = split(found * gain_ref[...])
    for at in chunks(n * n, DEEP):
        mixed[at, :] = matmul(xs[at, :], woh[...], wol[...])


def gradient_kernel(
    n, x_ref, y_ref, left, right, z_n, s1_n, s3_n, gate_n, z_f, s1_f, s3_f, gate_f, zown, rown,
    xhat, rstds, xs, mixed, gain_ref, out_gain_ref, own, other, wnh, wnl, wqh, wql,
    up_ref, dp_ref, dig_ref, dog_ref, de_ref, dg_ref, do_ref, ms, dh, dl, upd, hidden, dtri, d_left, d_right, grads,
):
    c, s = LANES, LANES // 2
    blk = up_ref.shape[0]
    q = blk // n
    upper = x_ref.shape[0] // (2 * blk)
    chan = lax.axis_index("chan")
    half = blk // 2
    part = n * n // 2
    sides = ((x_ref, gate_n), (y_ref, gate_f))

    for k, (ref, gate) in enumerate(sides):
        for b, ct in enumerate(cells_from(ref, blk, upper, chan)):
            here, there = slice(b * half, (b + 1) * half), slice(k * part + b * half, k * part + (b + 1) * half)
            a, mix = gate[here, :], mixed[there, :]
            dm = ct * a
            ms[there, :c], ms[there, c:] = split(dm)
            dh[there, 4 * c :], dl[there, 4 * c :] = split(dm * mix * (1.0 - a))
            if k == 0 and b < 2:
                upd[here, :] = a * mix
    for at in chunks(n * n, DEEP):
        hidden[at, :] = matmul(ms[at, :], wqh[...], wql[...])
    total = jnp.zeros((8, c), F32)
    for at in chunks(n * n):
        found, ng = xhat[at, :], hidden[at, :] * out_gain_ref[...]
        dtri[at, :] = rstds[at, :] * (ng - mean_lanes(ng) - found * mean_lanes(ng * found))
        total = total + jnp.sum((found * hidden[at, :]).reshape(-1, 8, c), axis=0)
    dog_ref[...] = jnp.sum(total, axis=0, keepdims=True)[:, :s]

    held = [pl.multiple_of(held_row(m, q, upper, n) * n, n) for m in range(n)]

    def of_left(first):
        return products(n, lambda a, m: row_of(dtri, (first + a) * n + m), lambda m: right[pl.ds(held[m], n), :])

    def of_right(first):
        mine = [true_row(first + a, q, upper, n) for a in range(ROWS)]
        return products(n, lambda a, m: row_of(dtri, m * n + mine[a]), lambda m: left[m * n : (m + 1) * n, :])

    over_rows(n, d_left, of_left)
    over_rows(n, d_right, of_right)
    for k, (s1, s3) in enumerate(((s1_n, s3_n), (s1_f, s3_f))):
        for here in chunks(part):
            at = slice(k * part + here.start, k * part + here.stop)
            d, a = d_left[at, :], s1[here, :]
            dh[at, :c], dl[at, :c] = split(d * a)
            dh[at, c : 2 * c], dl[at, c : 2 * c] = split(d * left[at, :] * (1.0 - a))
            d, a = d_right[at, :], s3[here, :]
            dh[at, 2 * c : 3 * c], dl[at, 2 * c : 3 * c] = split(d * a)
            dh[at, 3 * c : 4 * c], dl[at, 3 * c : 4 * c] = split(d * right[at, :] * (1.0 - a))

    def turned(at, z):
        zt = z[...].T
        wide = dot(zt, dh[at, :])
        return wide[:c] + (wide[c:] + dot(zt[:c], dl[at, :]))

    def joined(high, low, b):
        wide = down(high, b)
        return wide[:, :c] + (wide[:, c:] + down(low, b[:, :c]))

    grads[...] = (turned(slice(0, part), z_n) + turned(slice(part, 2 * part), z_f)).T
    do_ref[...] = joined(xs[:, :s], xs[:, c : c + s], ms[...])

    gain = gain_ref[...]
    mine = pl.ds(pl.multiple_of(4 * c + s * chan, s), s)
    others = pl.ds(pl.multiple_of(4 * c + s * (1 - chan), s), s)
    dg_ref[...] = grads[mine, :] * gain
    weighted = own[4 * s : 5 * s, :] * grads[mine, :] + other[4 * s : 5 * s, :] * grads[others, :]
    for e in range(4):
        mine, others = grads[e * c : e * c + s, :], grads[e * c + s : (e + 1) * c, :]
        de_ref[e] = mine * gain
        at = slice(e * s, (e + 1) * s)
        weighted = weighted + own[at, :] * mine + other[at, :] * others
    d_gain = jnp.sum(weighted, axis=0, keepdims=True)

    def own_half(x):
        return jnp.where(chan == 0, x[:, :s], pltpu.roll(x, s, 1)[:, :s])

    dig_ref[...] = own_half(jnp.broadcast_to(d_gain, (8, c)))[:1]
    up_ref[...] = own_half(upd[...])
    dz = dot(dh[:blk, :], wnh[...]) + (dot(dh[:blk, :], wnl[...]) + dot(dl[:blk, :], wnh[...]))
    zhat = zown[...]
    dp_ref[...] = own_half(rown[...] * (dz - mean_lanes(dz) - zhat * mean_lanes(dz * zhat)))


def rest_kernel(
    n, blk, x_ref, y_ref, pair_ref, z_n, left_n, s1_n, right_n, s3_n, gate_n, zown, rown, gain_ref, out_gain_ref, own,
    other, wnh, wnl, wdh, wtl, woh, wol, wqh, wql, up_ref, dp_ref, dig_ref, dog_ref, de_ref, dg_ref, do_ref,
    left, right, z_f, s1_f, s3_f, gate_f, xhat, rstds, xs, mixed, right_t, tri, proj, *scratch,
):
    q, upper, part = blk // n, x_ref.shape[0] // (2 * blk), n * n // 2
    left[:part, :], right[:part, :] = left_n[...], right_n[...]
    left_f, right_f = left.at[pl.ds(part, part)], right.at[pl.ds(part, part)]
    project_kernel(blk, pair_ref, wdh, wtl, z_f, left_f, s1_f, right_f, s3_f, gate_f, None, None, proj)
    triangle_kernel(n, q, upper, left, right, out_gain_ref, woh, wol, xhat, rstds, xs, mixed, right_t, tri)
    gradient_kernel(
        n, x_ref, y_ref, left, right, z_n, s1_n, s3_n, gate_n, z_f, s1_f, s3_f, gate_f, zown, rown,
        xhat, rstds, xs, mixed, gain_ref, out_gain_ref, own, other, wnh, wnl, wqh, wql,
        up_ref, dp_ref, dig_ref, dog_ref, de_ref, dg_ref, do_ref, *scratch,
    )


def call(kernel, name, out, scratch, limit, flops, *args):
    vm = pl.BlockSpec(memory_space=pltpu.VMEM)
    return pl.pallas_call(
        kernel,
        out_shape=[jax.ShapeDtypeStruct(shape, dtype) for shape, dtype in out],
        in_specs=[vm] * len(args),
        out_specs=[vm] * len(out),
        scratch_shapes=[pltpu.VMEM(shape, dtype) for shape, dtype in scratch],
        compiler_params=pltpu.CompilerParams(vmem_limit_bytes=limit << 20),
        cost_estimate=pl.CostEstimate(flops=flops, bytes_accessed=1 << 10, transcendentals=0),
        name=name,
    )(*args)


def gathered(devices, pair, in_gain, output_gain, w_edges, w_gate, w_out, cotangent):
    s, q, n = pair.shape
    c = 2 * s
    blk = q * n
    cells = n * n
    upper = devices // 8

    def swap(x, bits):
        return lax.ppermute(x, ("row", "chan"), [(i, i ^ bits) for i in range(devices)])

    def packed(x):
        x = jnp.transpose(x, (1, 2, 0)).reshape(2, blk // 2, s)
        return jnp.concatenate([x[0], x[1]], axis=1)[None]

    w_e = jnp.transpose(w_edges, (0, 2, 1))
    w_g = jnp.transpose(w_gate)
    held = jnp.concatenate([packed(pair), packed(cotangent)])
    gain_row = jnp.pad(output_gain[None], ((0, 7), (0, s)))
    held = lax.optimization_barrier(held)
    held = jnp.where(lax.axis_index("chan") == 0, held, jnp.concatenate([held[..., s:], held[..., :s]], axis=-1))
    (mine,) = call(pack_kernel, "pack", [((6 * s + 8, c), F32)], [], 8, 1 << 20, w_e, w_g, w_out, gain_row)
    held = jnp.concatenate([held] + [swap(held, 8 * apart) for apart in range(1, upper)], axis=1)
    other = swap(mine, 1)
    held, mine = lax.optimization_barrier((held, mine))
    parts = [swap(held, bits) for bits in (1, 4, 5)]

    gain = in_gain[None]
    wnh, wnl, wdh, wtl, woh, wol, wqh, wql, out_gain = call(
        prepare_kernel,
        "prepare",
        [(x, BF16) for x in [(5 * c, c), (5 * c, c), (2 * c, 5 * c), (c, 5 * c), (2 * c, c), (c, c), (2 * c, c), (c, c)]]
        + [((1, c), F32)],
        [],
        8,
        1 << 20,
        gain, mine, other,
    )
    parts, wdh = lax.optimization_barrier((parts, wdh))
    held = jnp.concatenate([held, *parts[::-1]], axis=1)
    pairs, cots = held[0], held[1]
    pairs_far = swap(pairs, 2)
    cots_far = swap(cots, 2)

    full, both, wide = ((cells, c), F32), ((cells, 2 * c), BF16), ((cells, 5 * c), BF16)
    part, own = ((cells // 2, c), F32), ((blk, c), F32)
    half, many = [((cells // 2, 2 * c), BF16)] + [part] * 5, ((cells // 2, 5 * c), F32)
    near = call(
        functools.partial(project_kernel, blk), "project", half + [own] * 2, [many], 16, 1 << 30, pairs, wdh, wtl
    )
    up, dp, dig, dog, de, dg, do = call(
        functools.partial(rest_kernel, n, blk),
        "rest",
        [(x, F32) for x in [(blk, s), (blk, s), (1, s), (1, s), (4, s, c), (s, c), (s, c)]],
        [full, full] + half[:1] + [part] * 3 + [full, full, both, full, full, full, many]
        + [both, wide, wide, own] + [full] * 4 + [((5 * c, c), F32)],
        32,
        1 << 33,
        cots, cots_far, pairs_far, *near, gain, out_gain, mine, other, wnh, wnl, wdh, wtl, woh, wol, wqh, wql,
    )

    def pair_of(x):
        return jnp.transpose(x.reshape(q, n, s), (2, 0, 1))

    return (pair_of(up), pair_of(dp), dig[0], dog[0], jnp.transpose(de, (0, 2, 1)), jnp.transpose(dg), do)


def solution(mesh):
    devices, chans = mesh.size, mesh.shape["chan"]

    def shards(pair, in_gain, output_gain, w_edges, *rest):
        n, c = pair.shape[2], w_edges.shape[1]
        fits = (
            chans == 2 and devices >= 8 and devices & (devices - 1) == 0 and n <= 32 and n % 16 == 0
            and c == LANES and w_edges.shape[2] * chans == LANES and (pair.shape[1] * n) % 32 == 0
        )
        step = functools.partial(gathered, devices) if fits else spread
        return step(pair, in_gain, output_gain, w_edges, *rest)

    placed = (
        P("chan", "row", None),
        P(),
        P("chan"),
        P(None, None, "chan"),
        P(None, "chan"),
        P("chan", None),
        P("chan", "row", None),
    )
    return jax.shard_map(
        shards,
        mesh=mesh,
        in_specs=placed,
        out_specs=(placed[0], placed[0], P("chan"), P("chan"), placed[3], placed[4], placed[5]),
        check_vma=False,
    )
```

```python
import functools

import jax
import jax.numpy as jnp
from jax import lax
from jax.experimental import pallas as pl
from jax.experimental.pallas import tpu as pltpu
from jax.sharding import PartitionSpec as P

HIDDEN_WIDTH = 128
EPS = 1e-05
F32 = jnp.float32
BF16 = jnp.bfloat16
LANES = 128
ROWS = 16
CHUNK = 64
DEEP = 256


def spread(pair, in_gain, output_gain, w_edges, w_gate, w_out, cotangent):
    hp = lax.Precision.HIGHEST
    shard_c = pair.shape[0]
    whole = lax.all_gather(pair, "chan", axis=0, tiled=True)
    centred = whole - jnp.mean(whole, 0)
    pair_rstd = lax.rsqrt(jnp.mean(centred * centred, 0) + 1e-05)
    zhat = centred * pair_rstd
    normed = zhat * in_gain[:, None, None]
    proj = jnp.einsum("ech,crn->ehrn", w_edges, normed, precision=hp)
    left_sig = jax.nn.sigmoid(proj[1])
    left = left_sig * proj[0]
    right_sig = jax.nn.sigmoid(proj[3])
    right = right_sig * proj[2]
    gate = jax.nn.sigmoid(jnp.einsum("dc,drn->crn", w_gate, normed, precision=hp))
    right_all = lax.all_gather(right, "row", axis=1, tiled=True)
    triangle_product = jnp.einsum("hrk,hjk->hrj", left, right_all, precision=hp)
    first, second = lax.psum(
        (jnp.sum(triangle_product, 0), jnp.sum(triangle_product * triangle_product, 0)), "chan"
    )
    hidden_average = first / HIDDEN_WIDTH
    hidden_inverse_deviation = lax.rsqrt(
        second / HIDDEN_WIDTH - hidden_average * hidden_average + 1e-05
    )
    normalized_hidden = (triangle_product - hidden_average) * hidden_inverse_deviation
    hidden_state = normalized_hidden * output_gain[:, None, None]
    mixed = lax.psum_scatter(
        jnp.einsum("hc,hrn->crn", w_out, hidden_state, precision=hp),
        "chan",
        scatter_dimension=0,
        tiled=True,
    )
    update = gate * mixed
    d_mixed = cotangent * gate
    d_gate_pre = cotangent * mixed * gate * (1.0 - gate)
    d_mixed_all = lax.all_gather(d_mixed, "chan", axis=0, tiled=True)
    hidden_gradient = jnp.einsum("hc,crn->hrn", w_out, d_mixed_all, precision=hp)
    g_out = jnp.einsum("hrn,crn->hc", hidden_state, d_mixed_all, precision=hp)
    output_gain_gradient = jnp.sum(normalized_hidden * hidden_gradient, (1, 2))
    normalized_gradient = hidden_gradient * output_gain[:, None, None]
    first_average_term, second_average_term = lax.psum(
        (jnp.sum(normalized_gradient, 0), jnp.sum(normalized_gradient * normalized_hidden, 0)),
        "chan",
    )
    triangle_gradient = hidden_inverse_deviation * (
        normalized_gradient
        - first_average_term / HIDDEN_WIDTH
        - normalized_hidden * (second_average_term / HIDDEN_WIDTH)
    )
    d_tri_cols = lax.all_to_all(triangle_gradient, "row", split_axis=2, concat_axis=1, tiled=True)
    d_left = jnp.einsum("hrj,hjk->hrk", triangle_gradient, right_all, precision=hp)
    d_right = jnp.einsum(
        "hij,hik->hjk", d_tri_cols, lax.all_gather(left, "row", axis=1, tiled=True), precision=hp
    )
    d_proj = jnp.stack(
        [
            d_left * left_sig,
            d_left * proj[0] * left_sig * (1.0 - left_sig),
            d_right * right_sig,
            d_right * proj[2] * right_sig * (1.0 - right_sig),
        ]
    )
    g_edges = jnp.einsum("crn,ehrn->ech", normed, d_proj, precision=hp)
    g_gate = jnp.einsum("drn,crn->dc", normed, d_gate_pre, precision=hp)
    offset = lax.axis_index("chan") * shard_c
    first_part = jnp.einsum("ech,ehrn->crn", w_edges, d_proj, precision=hp)
    d_normed = lax.psum(
        first_part + jnp.einsum("dc,crn->drn", w_gate, d_gate_pre, precision=hp), "chan"
    )
    d_zhat = d_normed * in_gain[:, None, None]
    first_mean = jnp.mean(d_zhat, 0)
    second_mean = jnp.mean(d_zhat * zhat, 0)
    d_full = pair_rstd * (d_zhat - first_mean - zhat * second_mean)
    d_pair = lax.dynamic_slice_in_dim(d_full, offset, shard_c, 0)
    g_in_gain = lax.dynamic_slice_in_dim(jnp.sum(zhat * d_normed, (1, 2)), offset, shard_c, 0)
    totals = lax.psum((g_in_gain, output_gain_gradient, g_edges, g_gate, g_out), "row")
    return (update, d_pair, totals[0], totals[1], totals[2], totals[3], totals[4])


def split(x):
    hi = x.astype(BF16)
    return hi, (x - hi.astype(F32)).astype(BF16)


def dot(a, b):
    return jnp.dot(a, b, preferred_element_type=F32)


def matmul(a, twice_high, low):
    return dot(a, twice_high) + dot(a[:, :LANES], low)


def down(a, b):
    return lax.dot_general(a, b, (((0,), (0,)), ((), ())), preferred_element_type=F32)


def chunks(cells, step=CHUNK):
    return [slice(at, at + step) for at in range(0, cells, step)]


def mean_lanes(x):
    return jnp.mean(x, axis=-1, keepdims=True)


def norm_lanes(x):
    centred = x - mean_lanes(x)
    rstd = lax.rsqrt(mean_lanes(centred * centred) + EPS)
    return centred * rstd, rstd


def cells_from(ref, blk, upper, chan):
    half = blk // 2
    low = lax.broadcasted_iota(jnp.int32, (half, LANES), 1) < LANES // 2
    for t in range(2 * upper):
        own, other = ((0, 3), (2, 1))[t // upper]

        def block(side):
            at = (t % upper + upper * (own + (other - own) * side)) * half
            return ref[pl.ds(pl.multiple_of(at, half), half), :]

        first, second = block(chan), block(1 - chan)
        yield jnp.where(low, first, second)
        yield pltpu.roll(jnp.where(low, second, first), LANES // 2, 1)


def true_row(p, q, upper, rows):
    row = lax.axis_index("row")
    far, t = p // (rows // 2), p % (rows // 2) // q
    return (((row // 2) ^ (t % upper * 2 + t // upper)) * 2 + ((row % 2) ^ far)) * q + p % q


def pack_kernel(we, wg, wo, gain, mine):
    s = wg.shape[0]
    for e in range(4):
        mine[e * s : (e + 1) * s, :] = we[e]
    mine[4 * s : 5 * s, :] = wg[...]
    mine[5 * s : 6 * s, :] = wo[...]
    mine[6 * s :, :] = gain[...]


def prepare_kernel(gain_ref, mine, other, wnh, wnl, wdh, wtl, woh, wol, wqh, wql, gain_out):
    c = LANES
    s = c // 2
    chan = lax.axis_index("chan")
    gain = gain_ref[...]

    def both(k):
        at = slice(k * s, (k + 1) * s)
        return mine[at, :], other[at, :]

    def put(k, whole):
        at = slice(k * c, (k + 1) * c)
        wnh[at, :], wnl[at, :] = split(whole)
        high, wtl[:, at] = split(whole.T)
        wdh[:c, at] = high
        wdh[c:, at] = high

    for e in range(4):
        put(e, jnp.concatenate(both(e), axis=0) * gain)
    a, b = both(4)
    put(4, jnp.concatenate([jnp.where(chan == 0, a, b), jnp.where(chan == 0, b, a)], axis=0) * gain)
    whole = jnp.concatenate(both(5), axis=0)
    high, wol[...] = split(whole)
    woh[:c, :] = high
    woh[c:, :] = high
    high, wql[...] = split(whole.T)
    wqh[:c, :] = high
    wqh[c:, :] = high
    gain_out[:, :s] = mine[6 * s : 6 * s + 1, :s]
    gain_out[:, s:] = other[6 * s : 6 * s + 1, :s]


def project_kernel(blk, whole, wdh, wtl, z, left, s1, right, s3, gate, zown, rown, ct, proj):
    c = LANES
    x_ref = whole.at[0]
    upper = x_ref.shape[0] // (2 * blk)
    chan = lax.axis_index("chan")
    half = blk // 2
    if ct is not None:
        for k, cells in enumerate(cells_from(whole.at[1], blk, upper, chan)):
            ct[k * half : (k + 1) * half, :] = cells
    for k, cells in enumerate(cells_from(x_ref, blk, upper, chan)):
        at = slice(k * half, (k + 1) * half)
        zhat, rstd = norm_lanes(cells)
        z[at, :c], z[at, c:] = split(zhat)
        if k < 2 and zown is not None:
            zown[at, :] = zhat
            rown[at, :] = jnp.broadcast_to(rstd, zhat.shape)
    for at in chunks(z.shape[0], DEEP):
        proj[at, :] = matmul(z[at, :], wdh[...], wtl[...])
    for at in chunks(z.shape[0]):
        a = jax.nn.sigmoid(proj[at, c : 2 * c])
        left[at, :], s1[at, :] = a * proj[at, :c], a
        a = jax.nn.sigmoid(proj[at, 3 * c : 4 * c])
        right[at, :], s3[at, :] = a * proj[at, 2 * c : 3 * c], a
        gate[at, :] = jax.nn.sigmoid(proj[at, 4 * c :])


def products(n, x_row, y_of):
    acc = [jnp.zeros((n // 8, 8, LANES), F32) for _ in range(ROWS)]
    for m in range(n):
        y = y_of(m).reshape(n // 8, 8, LANES)
        for a in range(ROWS):
            acc[a] = acc[a] + x_row(a, m)[None] * y
    return jnp.concatenate([part.reshape(n, LANES) for part in acc], axis=0)


def row_of(ref, at):
    return ref[pl.ds(at, 8, stride=0), :]


def over_rows(n, out, body):
    def some(b, carry):
        out[pl.ds(pl.multiple_of(b * ROWS * n, ROWS * n), ROWS * n), :] = body(b * ROWS)
        return carry

    lax.fori_loop(0, n // ROWS, some, 0)


def triangle_kernel(n, q, upper, left, sides, gain_ref, woh, wol, xhat, rstds, xs, mixed, right, right_t, tri):
    c = LANES
    for p in range(n):
        ref, at = sides[p // (n // 2)], p % (n // 2) * n
        right[pl.ds(pl.multiple_of(true_row(p, q, upper, n) * n, n), n), :] = ref[at : at + n, :]
    right_t[...] = jnp.swapaxes(right[...].reshape(n, n, c), 0, 1).reshape(n * n, c)

    def body(first):
        return products(
            n, lambda a, m: row_of(left, (first + a) * n + m), lambda m: right_t[m * n : (m + 1) * n, :]
        )

    over_rows(n, tri, body)
    for at in chunks(n * n):
        found, rstd = norm_lanes(tri[at, :])
        xhat[at, :] = found
        rstds[at, :] = jnp.broadcast_to(rstd, found.shape)
        xs[at, :c], xs[at, c:] = split(found * gain_ref[...])
    for at in chunks(n * n, DEEP):
        mixed[at, :] = matmul(xs[at, :], woh[...], wol[...])


def gradient_kernel(
    n, ct_n, y_ref, left, right, z_n, s1_n, right_n, s3_n, gate_n, z_f, s1_f, right_f, s3_f, gate_f, zown, rown,
    xhat, rstds, xs, mixed, gain_ref, out_gain_ref, own, other, wnh, wnl, wqh, wql,
    up_ref, dp_ref, dig_ref, dog_ref, de_ref, dg_ref, do_ref, ms, dh, dl, upd, hidden, dtri, d_left, d_right, grads,
):
    c, s = LANES, LANES // 2
    blk = up_ref.shape[0]
    q = blk // n
    y_ref = y_ref.at[1]
    upper = y_ref.shape[0] // (2 * blk)
    chan = lax.axis_index("chan")
    half = blk // 2
    part = n * n // 2
    near = (ct_n[at, :] for at in chunks(part, half))
    sides = ((near, gate_n), (cells_from(y_ref, blk, upper, chan), gate_f))

    for k, (cells, gate) in enumerate(sides):
        for b, ct in enumerate(cells):
            here, there = slice(b * half, (b + 1) * half), slice(k * part + b * half, k * part + (b + 1) * half)
            a, mix = gate[here, :], mixed[there, :]
            dm = ct * a
            ms[there, :c], ms[there, c:] = split(dm)
            dh[there, 4 * c :], dl[there, 4 * c :] = split(dm * mix * (1.0 - a))
            if k == 0 and b < 2:
                upd[here, :] = a * mix
    for at in chunks(n * n, DEEP):
        hidden[at, :] = matmul(ms[at, :], wqh[...], wql[...])
    total = jnp.zeros((8, c), F32)
    for at in chunks(n * n):
        found, ng = xhat[at, :], hidden[at, :] * out_gain_ref[...]
        dtri[at, :] = rstds[at, :] * (ng - mean_lanes(ng) - found * mean_lanes(ng * found))
        total = total + jnp.sum((found * hidden[at, :]).reshape(-1, 8, c), axis=0)
    dog_ref[...] = jnp.sum(total, axis=0, keepdims=True)[:, :s]

    def of_left(first):
        return products(n, lambda a, m: row_of(dtri, (first + a) * n + m), lambda m: right[m * n : (m + 1) * n, :])

    def of_right(first):
        mine = [true_row(first + a, q, upper, n) for a in range(ROWS)]
        return products(n, lambda a, m: row_of(dtri, m * n + mine[a]), lambda m: left[m * n : (m + 1) * n, :])

    over_rows(n, d_left, of_left)
    over_rows(n, d_right, of_right)
    for k, (s1, edge, s3) in enumerate(((s1_n, right_n, s3_n), (s1_f, right_f, s3_f))):
        for here in chunks(part):
            at = slice(k * part + here.start, k * part + here.stop)
            d, a = d_left[at, :], s1[here, :]
            dh[at, :c], dl[at, :c] = split(d * a)
            dh[at, c : 2 * c], dl[at, c : 2 * c] = split(d * left[at, :] * (1.0 - a))
            d, a = d_right[at, :], s3[here, :]
            dh[at, 2 * c : 3 * c], dl[at, 2 * c : 3 * c] = split(d * a)
            dh[at, 3 * c : 4 * c], dl[at, 3 * c : 4 * c] = split(d * edge[here, :] * (1.0 - a))

    def turned(at, z):
        zt = z[...].T
        wide = dot(zt, dh[at, :])
        return wide[:c] + (wide[c:] + dot(zt[:c], dl[at, :]))

    def joined(high, low, b):
        wide = down(high, b)
        return wide[:, :c] + (wide[:, c:] + down(low, b[:, :c]))

    grads[...] = (turned(slice(0, part), z_n) + turned(slice(part, 2 * part), z_f)).T
    do_ref[...] = joined(xs[:, :s], xs[:, c : c + s], ms[...])

    gain = gain_ref[...]
    mine = pl.ds(pl.multiple_of(4 * c + s * chan, s), s)
    others = pl.ds(pl.multiple_of(4 * c + s * (1 - chan), s), s)
    dg_ref[...] = grads[mine, :] * gain
    weighted = own[4 * s : 5 * s, :] * grads[mine, :] + other[4 * s : 5 * s, :] * grads[others, :]
    for e in range(4):
        mine, others = grads[e * c : e * c + s, :], grads[e * c + s : (e + 1) * c, :]
        de_ref[e] = mine * gain
        at = slice(e * s, (e + 1) * s)
        weighted = weighted + own[at, :] * mine + other[at, :] * others
    d_gain = jnp.sum(weighted, axis=0, keepdims=True)

    def own_half(x):
        return jnp.where(chan == 0, x[:, :s], pltpu.roll(x, s, 1)[:, :s])

    dig_ref[...] = own_half(jnp.broadcast_to(d_gain, (8, c)))[:1]
    up_ref[...] = own_half(upd[...])
    dz = dot(dh[:blk, :], wnh[...]) + (dot(dh[:blk, :], wnl[...]) + dot(dl[:blk, :], wnh[...]))
    zhat = zown[...]
    dp_ref[...] = own_half(rown[...] * (dz - mean_lanes(dz) - zhat * mean_lanes(dz * zhat)))


def rest_kernel(
    n, blk, y_ref, z_n, left_n, s1_n, right_n, s3_n, gate_n, zown, rown, ct_n, gain_ref, out_gain_ref, own,
    other, wnh, wnl, wdh, wtl, woh, wol, wqh, wql, up_ref, dp_ref, dig_ref, dog_ref, de_ref, dg_ref, do_ref,
    left, right, z_f, s1_f, right_f, s3_f, gate_f, xhat, rstds, xs, mixed, right_t, tri, proj, *scratch,
):
    q, upper, part = blk // n, y_ref.shape[1] // (2 * blk), n * n // 2
    left[:part, :] = left_n[...]
    left_f = left.at[pl.ds(part, part)]
    project_kernel(blk, y_ref, wdh, wtl, z_f, left_f, s1_f, right_f, s3_f, gate_f, None, None, None, proj)
    sides = (right_n, right_f)
    triangle_kernel(n, q, upper, left, sides, out_gain_ref, woh, wol, xhat, rstds, xs, mixed, right, right_t, tri)
    gradient_kernel(
        n, ct_n, y_ref, left, right, z_n, s1_n, right_n, s3_n, gate_n, z_f, s1_f, right_f, s3_f, gate_f, zown, rown,
        xhat, rstds, xs, mixed, gain_ref, out_gain_ref, own, other, wnh, wnl, wqh, wql,
        up_ref, dp_ref, dig_ref, dog_ref, de_ref, dg_ref, do_ref, *scratch,
    )


def call(kernel, name, out, scratch, limit, flops, *args):
    vm = pl.BlockSpec(memory_space=pltpu.VMEM)
    return pl.pallas_call(
        kernel,
        out_shape=[jax.ShapeDtypeStruct(shape, dtype) for shape, dtype in out],
        in_specs=[vm] * len(args),
        out_specs=[vm] * len(out),
        scratch_shapes=[pltpu.VMEM(shape, dtype) for shape, dtype in scratch],
        compiler_params=pltpu.CompilerParams(vmem_limit_bytes=limit << 20),
        cost_estimate=pl.CostEstimate(flops=flops, bytes_accessed=1 << 10, transcendentals=0),
        name=name,
    )(*args)


def gathered(devices, pair, in_gain, output_gain, w_edges, w_gate, w_out, cotangent):
    s, q, n = pair.shape
    c = 2 * s
    blk = q * n
    cells = n * n
    upper = devices // 8

    def swap(x, bits):
        return lax.ppermute(x, ("row", "chan"), [(i, i ^ bits) for i in range(devices)])

    def packed(x):
        x = jnp.transpose(x, (1, 2, 0)).reshape(2, blk // 2, s)
        return jnp.concatenate([x[0], x[1]], axis=1)[None]

    w_e = jnp.transpose(w_edges, (0, 2, 1))
    w_g = jnp.transpose(w_gate)
    held = jnp.concatenate([packed(pair), packed(cotangent)])
    gain_row = jnp.pad(output_gain[None], ((0, 7), (0, s)))
    held = lax.optimization_barrier(held)
    held = jnp.where(lax.axis_index("chan") == 0, held, jnp.concatenate([held[..., s:], held[..., :s]], axis=-1))
    (mine,) = call(pack_kernel, "pack", [((6 * s + 8, c), F32)], [], 8, 1 << 20, w_e, w_g, w_out, gain_row)
    held = jnp.concatenate([held] + [swap(held, 8 * apart) for apart in range(1, upper)], axis=1)
    other = swap(mine, 1)
    held, mine = lax.optimization_barrier((held, mine))
    parts = [swap(held, bits) for bits in (1, 4, 5)]

    gain = in_gain[None]
    wnh, wnl, wdh, wtl, woh, wol, wqh, wql, out_gain = call(
        prepare_kernel,
        "prepare",
        [(x, BF16) for x in [(5 * c, c), (5 * c, c), (2 * c, 5 * c), (c, 5 * c), (2 * c, c), (c, c), (2 * c, c), (c, c)]]
        + [((1, c), F32)],
        [],
        8,
        1 << 20,
        gain, mine, other,
    )
    parts, wdh = lax.optimization_barrier((parts, wdh))
    held = jnp.concatenate([held, *parts[::-1]], axis=1)
    far = swap(held, 2)

    full, both, wide = ((cells, c), F32), ((cells, 2 * c), BF16), ((cells, 5 * c), BF16)
    part, own = ((cells // 2, c), F32), ((blk, c), F32)
    half, many = [((cells // 2, 2 * c), BF16)] + [part] * 5, ((cells // 2, 5 * c), F32)
    near = call(
        functools.partial(project_kernel, blk), "project", half + [own] * 2 + [part], [many], 16, 1 << 30, held, wdh, wtl
    )
    up, dp, dig, dog, de, dg, do = call(
        functools.partial(rest_kernel, n, blk),
        "rest",
        [(x, F32) for x in [(blk, s), (blk, s), (1, s), (1, s), (4, s, c), (s, c), (s, c)]],
        [full, full] + half[:1] + [part] * 4 + [full, full, both, full, full, full, many]
        + [both, wide, wide, own] + [full] * 4 + [((5 * c, c), F32)],
        32,
        1 << 33,
        far, *near, gain, out_gain, mine, other, wnh, wnl, wdh, wtl, woh, wol, wqh, wql,
    )

    def pair_of(x):
        return jnp.transpose(x.reshape(q, n, s), (2, 0, 1))

    return (pair_of(up), pair_of(dp), dig[0], dog[0], jnp.transpose(de, (0, 2, 1)), jnp.transpose(dg), do)


def solution(mesh):
    devices, chans = mesh.size, mesh.shape["chan"]

    def shards(pair, in_gain, output_gain, w_edges, *rest):
        n, c = pair.shape[2], w_edges.shape[1]
        fits = (
            chans == 2 and devices >= 8 and devices & (devices - 1) == 0 and n <= 32 and n % 16 == 0
            and c == LANES and w_edges.shape[2] * chans == LANES and (pair.shape[1] * n) % 32 == 0
        )
        step = functools.partial(gathered, devices) if fits else spread
        return step(pair, in_gain, output_gain, w_edges, *rest)

    placed = (
        P("chan", "row", None),
        P(),
        P("chan"),
        P(None, None, "chan"),
        P(None, "chan"),
        P("chan", None),
        P("chan", "row", None),
    )
    return jax.shard_map(
        shards,
        mesh=mesh,
        in_specs=placed,
        out_specs=(placed[0], placed[0], P("chan"), P("chan"), placed[3], placed[4], placed[5]),
        check_vma=False,
    )
```

```python
import functools

import jax
import jax.numpy as jnp
from jax import lax
from jax.experimental import pallas as pl
from jax.experimental.pallas import tpu as pltpu
from jax.sharding import PartitionSpec as P

HIDDEN_WIDTH = 128
EPS = 1e-05
F32 = jnp.float32
BF16 = jnp.bfloat16
LANES = 128
ROWS = 16
CHUNK = 64
DEEP = 256


def spread(pair, in_gain, output_gain, w_edges, w_gate, w_out, cotangent):
    hp = lax.Precision.HIGHEST
    shard_c = pair.shape[0]
    whole = lax.all_gather(pair, "chan", axis=0, tiled=True)
    centred = whole - jnp.mean(whole, 0)
    pair_rstd = lax.rsqrt(jnp.mean(centred * centred, 0) + 1e-05)
    zhat = centred * pair_rstd
    normed = zhat * in_gain[:, None, None]
    proj = jnp.einsum("ech,crn->ehrn", w_edges, normed, precision=hp)
    left_sig = jax.nn.sigmoid(proj[1])
    left = left_sig * proj[0]
    right_sig = jax.nn.sigmoid(proj[3])
    right = right_sig * proj[2]
    gate = jax.nn.sigmoid(jnp.einsum("dc,drn->crn", w_gate, normed, precision=hp))
    right_all = lax.all_gather(right, "row", axis=1, tiled=True)
    triangle_product = jnp.einsum("hrk,hjk->hrj", left, right_all, precision=hp)
    first, second = lax.psum(
        (jnp.sum(triangle_product, 0), jnp.sum(triangle_product * triangle_product, 0)), "chan"
    )
    hidden_average = first / HIDDEN_WIDTH
    hidden_inverse_deviation = lax.rsqrt(
        second / HIDDEN_WIDTH - hidden_average * hidden_average + 1e-05
    )
    normalized_hidden = (triangle_product - hidden_average) * hidden_inverse_deviation
    hidden_state = normalized_hidden * output_gain[:, None, None]
    mixed = lax.psum_scatter(
        jnp.einsum("hc,hrn->crn", w_out, hidden_state, precision=hp),
        "chan",
        scatter_dimension=0,
        tiled=True,
    )
    update = gate * mixed
    d_mixed = cotangent * gate
    d_gate_pre = cotangent * mixed * gate * (1.0 - gate)
    d_mixed_all = lax.all_gather(d_mixed, "chan", axis=0, tiled=True)
    hidden_gradient = jnp.einsum("hc,crn->hrn", w_out, d_mixed_all, precision=hp)
    g_out = jnp.einsum("hrn,crn->hc", hidden_state, d_mixed_all, precision=hp)
    output_gain_gradient = jnp.sum(normalized_hidden * hidden_gradient, (1, 2))
    normalized_gradient = hidden_gradient * output_gain[:, None, None]
    first_average_term, second_average_term = lax.psum(
        (jnp.sum(normalized_gradient, 0), jnp.sum(normalized_gradient * normalized_hidden, 0)),
        "chan",
    )
    triangle_gradient = hidden_inverse_deviation * (
        normalized_gradient
        - first_average_term / HIDDEN_WIDTH
        - normalized_hidden * (second_average_term / HIDDEN_WIDTH)
    )
    d_tri_cols = lax.all_to_all(triangle_gradient, "row", split_axis=2, concat_axis=1, tiled=True)
    d_left = jnp.einsum("hrj,hjk->hrk", triangle_gradient, right_all, precision=hp)
    d_right = jnp.einsum(
        "hij,hik->hjk", d_tri_cols, lax.all_gather(left, "row", axis=1, tiled=True), precision=hp
    )
    d_proj = jnp.stack(
        [
            d_left * left_sig,
            d_left * proj[0] * left_sig * (1.0 - left_sig),
            d_right * right_sig,
            d_right * proj[2] * right_sig * (1.0 - right_sig),
        ]
    )
    g_edges = jnp.einsum("crn,ehrn->ech", normed, d_proj, precision=hp)
    g_gate = jnp.einsum("drn,crn->dc", normed, d_gate_pre, precision=hp)
    offset = lax.axis_index("chan") * shard_c
    first_part = jnp.einsum("ech,ehrn->crn", w_edges, d_proj, precision=hp)
    d_normed = lax.psum(
        first_part + jnp.einsum("dc,crn->drn", w_gate, d_gate_pre, precision=hp), "chan"
    )
    d_zhat = d_normed * in_gain[:, None, None]
    first_mean = jnp.mean(d_zhat, 0)
    second_mean = jnp.mean(d_zhat * zhat, 0)
    d_full = pair_rstd * (d_zhat - first_mean - zhat * second_mean)
    d_pair = lax.dynamic_slice_in_dim(d_full, offset, shard_c, 0)
    g_in_gain = lax.dynamic_slice_in_dim(jnp.sum(zhat * d_normed, (1, 2)), offset, shard_c, 0)
    totals = lax.psum((g_in_gain, output_gain_gradient, g_edges, g_gate, g_out), "row")
    return (update, d_pair, totals[0], totals[1], totals[2], totals[3], totals[4])


def split(x):
    hi = x.astype(BF16)
    return hi, (x - hi.astype(F32)).astype(BF16)


def dot(a, b):
    return jnp.dot(a, b, preferred_element_type=F32)


def matmul(a, twice_high, low):
    return dot(a, twice_high) + dot(a[:, :LANES], low)


def down(a, b):
    return lax.dot_general(a, b, (((0,), (0,)), ((), ())), preferred_element_type=F32)


def chunks(cells, step=CHUNK):
    return [slice(at, at + step) for at in range(0, cells, step)]


def mean_lanes(x):
    return jnp.mean(x, axis=-1, keepdims=True)


def norm_lanes(x):
    centred = x - mean_lanes(x)
    rstd = lax.rsqrt(mean_lanes(centred * centred) + EPS)
    return centred * rstd, rstd


def cells_from(k, own_ref, rest_ref, blk):
    half = blk // 2
    across = own_ref.shape[1]
    low = (lax.broadcasted_iota(jnp.int32, (half, LANES), 1) < LANES // 2) == (lax.axis_index("chan") == 0)
    for t in range(2 * across // half):
        at = t * half % across

        def rest(line, at=at):
            return rest_ref[k, line * across + at : line * across + at + half, :]

        if t * half < across:
            own, other = own_ref[k, at : at + half, :], rest(2)
        else:
            own, other = rest(1), rest(0)
        yield jnp.where(low, own, other)
        yield pltpu.roll(jnp.where(low, other, own), LANES // 2, 1)


def true_row(p, q, upper, rows):
    row = lax.axis_index("row")
    far, t = p // (rows // 2), p % (rows // 2) // q
    return (((row // 2) ^ ((upper - t % upper) % upper * 2 + t // upper)) * 2 + ((row % 2) ^ far)) * q + p % q


def pack_kernel(we, wg, wo, gain, mine):
    s = wg.shape[0]
    for e in range(4):
        mine[e * s : (e + 1) * s, :] = we[e]
    mine[4 * s : 5 * s, :] = wg[...]
    mine[5 * s : 6 * s, :] = wo[...]
    mine[6 * s :, :] = gain[...]


def prepare_kernel(gain_ref, mine, other, wnh, wnl, wdh, wtl, woh, wol, wqh, wql, gain_out):
    c = LANES
    s = c // 2
    chan = lax.axis_index("chan")
    gain = gain_ref[...]

    def both(k):
        at = slice(k * s, (k + 1) * s)
        return mine[at, :], other[at, :]

    def put(k, whole):
        at = slice(k * c, (k + 1) * c)
        wnh[at, :], wnl[at, :] = split(whole)
        high, wtl[:, at] = split(whole.T)
        wdh[:c, at] = high
        wdh[c:, at] = high

    for e in range(4):
        put(e, jnp.concatenate(both(e), axis=0) * gain)
    a, b = both(4)
    put(4, jnp.concatenate([jnp.where(chan == 0, a, b), jnp.where(chan == 0, b, a)], axis=0) * gain)
    whole = jnp.concatenate(both(5), axis=0)
    high, wol[...] = split(whole)
    woh[:c, :] = high
    woh[c:, :] = high
    high, wql[...] = split(whole.T)
    wqh[:c, :] = high
    wqh[c:, :] = high
    gain_out[:, :s] = mine[6 * s : 6 * s + 1, :s]
    gain_out[:, s:] = other[6 * s : 6 * s + 1, :s]


def project_kernel(blk, own_ref, rest_ref, wdh, wtl, z, left, s1, right, s3, gate, zown, rown, ct, proj):
    c = LANES
    half = blk // 2
    if ct is not None:
        for k, cells in enumerate(cells_from(1, own_ref, rest_ref, blk)):
            ct[k * half : (k + 1) * half, :] = cells
    for k, cells in enumerate(cells_from(0, own_ref, rest_ref, blk)):
        at = slice(k * half, (k + 1) * half)
        zhat, rstd = norm_lanes(cells)
        z[at, :c], z[at, c:] = split(zhat)
        if k < 2 and zown is not None:
            zown[at, :] = zhat
            rown[at, :] = jnp.broadcast_to(rstd, zhat.shape)
    for at in chunks(z.shape[0], DEEP):
        proj[at, :] = matmul(z[at, :], wdh[...], wtl[...])
    for at in chunks(z.shape[0]):
        a = jax.nn.sigmoid(proj[at, c : 2 * c])
        left[at, :], s1[at, :] = a * proj[at, :c], a
        a = jax.nn.sigmoid(proj[at, 3 * c : 4 * c])
        right[at, :], s3[at, :] = a * proj[at, 2 * c : 3 * c], a
        gate[at, :] = jax.nn.sigmoid(proj[at, 4 * c :])


def products(n, x_row, y_of):
    acc = [jnp.zeros((n // 8, 8, LANES), F32) for _ in range(ROWS)]
    for m in range(n):
        y = y_of(m).reshape(n // 8, 8, LANES)
        for a in range(ROWS):
            acc[a] = acc[a] + x_row(a, m)[None] * y
    return jnp.concatenate([part.reshape(n, LANES) for part in acc], axis=0)


def row_of(ref, at):
    return ref[pl.ds(at, 8, stride=0), :]


def over_rows(n, outs, bodies):
    def some(b, carry):
        here = pl.ds(pl.multiple_of(b * ROWS * n, ROWS * n), ROWS * n)
        for out, body in zip(outs, bodies, strict=True):
            out[here, :] = body(b * ROWS)
        return carry

    lax.fori_loop(0, n // ROWS, some, 0)


def triangle_kernel(n, q, upper, left, sides, gain_ref, woh, wol, xhat, rstds, xs, mixed, right, right_t, tri):
    c = LANES
    for p in range(n):
        ref, at = sides[p // (n // 2)], p % (n // 2) * n
        right[pl.ds(pl.multiple_of(true_row(p, q, upper, n) * n, n), n), :] = ref[at : at + n, :]
    right_t[...] = jnp.swapaxes(right[...].reshape(n, n, c), 0, 1).reshape(n * n, c)

    def body(first):
        return products(
            n, lambda a, m: row_of(left, (first + a) * n + m), lambda m: right_t[m * n : (m + 1) * n, :]
        )

    over_rows(n, (tri,), (body,))
    for at in chunks(n * n):
        found, rstd = norm_lanes(tri[at, :])
        xhat[at, :] = found
        rstds[at, :] = jnp.broadcast_to(rstd, found.shape)
        xs[at, :c], xs[at, c:] = split(found * gain_ref[...])
    for at in chunks(n * n, DEEP):
        mixed[at, :] = matmul(xs[at, :], woh[...], wol[...])


def gradient_kernel(
    n, ct_n, far_a, far_b, left, right, z_n, s1_n, right_n, s3_n, gate_n, z_f, s1_f, right_f, s3_f, gate_f, zown, rown,
    xhat, rstds, xs, mixed, gain_ref, out_gain_ref, own, other, wnh, wnl, wqh, wql,
    up_ref, dp_ref, dig_ref, dog_ref, de_ref, dg_ref, do_ref, ms, dh, dl, upd, hidden, dtri, d_left, d_right, grads,
):
    c, s = LANES, LANES // 2
    blk = up_ref.shape[0]
    q = blk // n
    upper = 2 * far_a.shape[1] // blk
    chan = lax.axis_index("chan")
    half = blk // 2
    part = n * n // 2
    near = (ct_n[at, :] for at in chunks(part, half))
    sides = ((near, gate_n), (cells_from(1, far_a, far_b, blk), gate_f))

    for k, (cells, gate) in enumerate(sides):
        for b, ct in enumerate(cells):
            here, there = slice(b * half, (b + 1) * half), slice(k * part + b * half, k * part + (b + 1) * half)
            a, mix = gate[here, :], mixed[there, :]
            dm = ct * a
            ms[there, :c], ms[there, c:] = split(dm)
            dh[there, 4 * c :], dl[there, 4 * c :] = split(dm * mix * (1.0 - a))
            if k == 0 and b < 2:
                upd[here, :] = a * mix
    for at in chunks(n * n, DEEP):
        hidden[at, :] = matmul(ms[at, :], wqh[...], wql[...])
    total = jnp.zeros((8, c), F32)
    for at in chunks(n * n):
        found, ng = xhat[at, :], hidden[at, :] * out_gain_ref[...]
        dtri[at, :] = rstds[at, :] * (ng - mean_lanes(ng) - found * mean_lanes(ng * found))
        total = total + jnp.sum((found * hidden[at, :]).reshape(-1, 8, c), axis=0)
    dog_ref[...] = jnp.sum(total, axis=0, keepdims=True)[:, :s]

    def of_left(first):
        return products(n, lambda a, m: row_of(dtri, (first + a) * n + m), lambda m: right[m * n : (m + 1) * n, :])

    def of_right(first):
        mine = [true_row(first + a, q, upper, n) for a in range(ROWS)]
        return products(n, lambda a, m: row_of(dtri, m * n + mine[a]), lambda m: left[m * n : (m + 1) * n, :])

    over_rows(n, (d_left, d_right), (of_left, of_right))
    for k, (s1, edge, s3) in enumerate(((s1_n, right_n, s3_n), (s1_f, right_f, s3_f))):
        for here in chunks(part):
            at = slice(k * part + here.start, k * part + here.stop)
            d, a = d_left[at, :], s1[here, :]
            dh[at, :c], dl[at, :c] = split(d * a)
            dh[at, c : 2 * c], dl[at, c : 2 * c] = split(d * left[at, :] * (1.0 - a))
            d, a = d_right[at, :], s3[here, :]
            dh[at, 2 * c : 3 * c], dl[at, 2 * c : 3 * c] = split(d * a)
            dh[at, 3 * c : 4 * c], dl[at, 3 * c : 4 * c] = split(d * edge[here, :] * (1.0 - a))

    def turned(at, z):
        zt = z[...].T
        wide = dot(zt, dh[at, :])
        return wide[:c] + (wide[c:] + dot(zt[:c], dl[at, :]))

    def joined(high, low, b):
        wide = down(high, b)
        return wide[:, :c] + (wide[:, c:] + down(low, b[:, :c]))

    grads[...] = (turned(slice(0, part), z_n) + turned(slice(part, 2 * part), z_f)).T
    do_ref[...] = joined(xs[:, :s], xs[:, c : c + s], ms[...])

    gain = gain_ref[...]
    mine = pl.ds(pl.multiple_of(4 * c + s * chan, s), s)
    others = pl.ds(pl.multiple_of(4 * c + s * (1 - chan), s), s)
    dg_ref[...] = grads[mine, :] * gain
    weighted = own[4 * s : 5 * s, :] * grads[mine, :] + other[4 * s : 5 * s, :] * grads[others, :]
    for e in range(4):
        mine, others = grads[e * c : e * c + s, :], grads[e * c + s : (e + 1) * c, :]
        de_ref[e] = mine * gain
        at = slice(e * s, (e + 1) * s)
        weighted = weighted + own[at, :] * mine + other[at, :] * others
    d_gain = jnp.sum(weighted, axis=0, keepdims=True)

    def own_half(x):
        return jnp.where(chan == 0, x[:, :s], pltpu.roll(x, s, 1)[:, :s])

    dig_ref[...] = own_half(jnp.broadcast_to(d_gain, (8, c)))[:1]
    up_ref[...] = own_half(upd[...])
    dz = dot(dh[:blk, :], wnh[...]) + (dot(dh[:blk, :], wnl[...]) + dot(dl[:blk, :], wnh[...]))
    zhat = zown[...]
    dp_ref[...] = own_half(rown[...] * (dz - mean_lanes(dz) - zhat * mean_lanes(dz * zhat)))


def rest_kernel(
    n, blk, far_a, far_b, z_n, left_n, s1_n, right_n, s3_n, gate_n, zown, rown, ct_n, gain_ref, out_gain_ref, own,
    other, wnh, wnl, wdh, wtl, woh, wol, wqh, wql, up_ref, dp_ref, dig_ref, dog_ref, de_ref, dg_ref, do_ref,
    left, right, z_f, s1_f, right_f, s3_f, gate_f, xhat, rstds, xs, mixed, right_t, tri, proj, *scratch,
):
    q, upper, part = blk // n, 2 * far_a.shape[1] // blk, n * n // 2
    left[:part, :] = left_n[...]
    left_f = left.at[pl.ds(part, part)]
    project_kernel(blk, far_a, far_b, wdh, wtl, z_f, left_f, s1_f, right_f, s3_f, gate_f, None, None, None, proj)
    sides = (right_n, right_f)
    triangle_kernel(n, q, upper, left, sides, out_gain_ref, woh, wol, xhat, rstds, xs, mixed, right, right_t, tri)
    gradient_kernel(
        n, ct_n, far_a, far_b, left, right, z_n, s1_n, right_n, s3_n, gate_n, z_f, s1_f, right_f, s3_f, gate_f, zown, rown,
        xhat, rstds, xs, mixed, gain_ref, out_gain_ref, own, other, wnh, wnl, wqh, wql,
        up_ref, dp_ref, dig_ref, dog_ref, de_ref, dg_ref, do_ref, *scratch,
    )


def call(kernel, name, out, scratch, limit, flops, *args):
    vm = pl.BlockSpec(memory_space=pltpu.VMEM)
    return pl.pallas_call(
        kernel,
        out_shape=[jax.ShapeDtypeStruct(shape, dtype) for shape, dtype in out],
        in_specs=[vm] * len(args),
        out_specs=[vm] * len(out),
        scratch_shapes=[pltpu.VMEM(shape, dtype) for shape, dtype in scratch],
        compiler_params=pltpu.CompilerParams(vmem_limit_bytes=limit << 20),
        cost_estimate=pl.CostEstimate(flops=flops, bytes_accessed=1 << 10, transcendentals=0),
        name=name,
    )(*args)


def gathered(devices, pair, in_gain, output_gain, w_edges, w_gate, w_out, cotangent):
    s, q, n = pair.shape
    c = 2 * s
    blk = q * n
    cells = n * n
    upper = devices // 8

    def swap(x, bits):
        return lax.ppermute(x, ("row", "chan"), [(i, i ^ bits) for i in range(devices)])

    def packed(x):
        x = jnp.transpose(x, (1, 2, 0)).reshape(2, blk // 2, s)
        return jnp.concatenate([x[0], x[1]], axis=1)[None]

    w_e = jnp.transpose(w_edges, (0, 2, 1))
    w_g = jnp.transpose(w_gate)
    held = jnp.concatenate([packed(pair), packed(cotangent)])
    gain_row = jnp.pad(output_gain[None], ((0, 7), (0, s)))
    held = lax.optimization_barrier(held)
    held = jnp.where(lax.axis_index("chan") == 0, held, jnp.concatenate([held[..., s:], held[..., :s]], axis=-1))
    (mine,) = call(pack_kernel, "pack", [((6 * s + 8, c), F32)], [], 8, 1 << 20, w_e, w_g, w_out, gain_row)
    held = jnp.concatenate([held] + [swap(held, 8 * apart) for apart in range(upper - 1, 0, -1)], axis=1)
    other = swap(mine, 1)
    held, mine = lax.optimization_barrier((held, mine))
    parts = [swap(held, bits) for bits in (5, 4, 1)]

    gain = in_gain[None]
    wnh, wnl, wdh, wtl, woh, wol, wqh, wql, out_gain = call(
        prepare_kernel,
        "prepare",
        [(x, BF16) for x in [(5 * c, c), (5 * c, c), (2 * c, 5 * c), (c, 5 * c), (2 * c, c), (c, c), (2 * c, c), (c, c)]]
        + [((1, c), F32)],
        [],
        8,
        1 << 20,
        gain, mine, other,
    )
    far_a = swap(held, 2)
    parts, wdh, far_a = lax.optimization_barrier((parts, wdh, far_a))
    others = jnp.concatenate(parts, axis=1)
    far_b = swap(others, 2)

    full, both, wide = ((cells, c), F32), ((cells, 2 * c), BF16), ((cells, 5 * c), BF16)
    part, own = ((cells // 2, c), F32), ((blk, c), F32)
    half, many = [((cells // 2, 2 * c), BF16)] + [part] * 5, ((cells // 2, 5 * c), F32)
    near = call(
        functools.partial(project_kernel, blk), "project", half + [own] * 2 + [part], [many], 16, 1 << 30, held, others, wdh, wtl
    )
    up, dp, dig, dog, de, dg, do = call(
        functools.partial(rest_kernel, n, blk),
        "rest",
        [(x, F32) for x in [(blk, s), (blk, s), (1, s), (1, s), (4, s, c), (s, c), (s, c)]],
        [full, full] + half[:1] + [part] * 4 + [full, full, both, full, full, full, many]
        + [both, wide, wide, own] + [full] * 4 + [((5 * c, c), F32)],
        32,
        1 << 33,
        far_a, far_b, *near, gain, out_gain, mine, other, wnh, wnl, wdh, wtl, woh, wol, wqh, wql,
    )

    def pair_of(x):
        return jnp.transpose(x.reshape(q, n, s), (2, 0, 1))

    return (pair_of(up), pair_of(dp), dig[0], dog[0], jnp.transpose(de, (0, 2, 1)), jnp.transpose(dg), do)


def solution(mesh):
    devices, chans = mesh.size, mesh.shape["chan"]

    def shards(pair, in_gain, output_gain, w_edges, *rest):
        n, c = pair.shape[2], w_edges.shape[1]
        fits = (
            chans == 2 and devices >= 8 and devices & (devices - 1) == 0 and n <= 32 and n * n % (2 * DEEP) == 0 and n % ROWS == 0
            and c == LANES and w_edges.shape[2] * chans == LANES and (pair.shape[1] * n) % 32 == 0
        )
        step = functools.partial(gathered, devices) if fits else spread
        return step(pair, in_gain, output_gain, w_edges, *rest)

    placed = (
        P("chan", "row", None),
        P(),
        P("chan"),
        P(None, None, "chan"),
        P(None, "chan"),
        P("chan", None),
        P("chan", "row", None),
    )
    return jax.shard_map(
        shards,
        mesh=mesh,
        in_specs=placed,
        out_specs=(placed[0], placed[0], P("chan"), P("chan"), placed[3], placed[4], placed[5]),
        check_vma=False,
    )
```

```python
import functools

import jax
import jax.numpy as jnp
from jax import lax
from jax.experimental import pallas as pl
from jax.experimental.pallas import tpu as pltpu
from jax.sharding import PartitionSpec as P

HIDDEN_WIDTH = 128
EPS = 1e-05
F32 = jnp.float32
BF16 = jnp.bfloat16
LANES = 128
ROWS = 16
CHUNK = 64
DEEP = 256


def spread(pair, in_gain, output_gain, w_edges, w_gate, w_out, cotangent):
    hp = lax.Precision.HIGHEST
    shard_c = pair.shape[0]
    whole = lax.all_gather(pair, "chan", axis=0, tiled=True)
    centred = whole - jnp.mean(whole, 0)
    pair_rstd = lax.rsqrt(jnp.mean(centred * centred, 0) + 1e-05)
    zhat = centred * pair_rstd
    normed = zhat * in_gain[:, None, None]
    proj = jnp.einsum("ech,crn->ehrn", w_edges, normed, precision=hp)
    left_sig = jax.nn.sigmoid(proj[1])
    left = left_sig * proj[0]
    right_sig = jax.nn.sigmoid(proj[3])
    right = right_sig * proj[2]
    gate = jax.nn.sigmoid(jnp.einsum("dc,drn->crn", w_gate, normed, precision=hp))
    right_all = lax.all_gather(right, "row", axis=1, tiled=True)
    triangle_product = jnp.einsum("hrk,hjk->hrj", left, right_all, precision=hp)
    first, second = lax.psum(
        (jnp.sum(triangle_product, 0), jnp.sum(triangle_product * triangle_product, 0)), "chan"
    )
    hidden_average = first / HIDDEN_WIDTH
    hidden_inverse_deviation = lax.rsqrt(
        second / HIDDEN_WIDTH - hidden_average * hidden_average + 1e-05
    )
    normalized_hidden = (triangle_product - hidden_average) * hidden_inverse_deviation
    hidden_state = normalized_hidden * output_gain[:, None, None]
    mixed = lax.psum_scatter(
        jnp.einsum("hc,hrn->crn", w_out, hidden_state, precision=hp),
        "chan",
        scatter_dimension=0,
        tiled=True,
    )
    update = gate * mixed
    d_mixed = cotangent * gate
    d_gate_pre = cotangent * mixed * gate * (1.0 - gate)
    d_mixed_all = lax.all_gather(d_mixed, "chan", axis=0, tiled=True)
    hidden_gradient = jnp.einsum("hc,crn->hrn", w_out, d_mixed_all, precision=hp)
    g_out = jnp.einsum("hrn,crn->hc", hidden_state, d_mixed_all, precision=hp)
    output_gain_gradient = jnp.sum(normalized_hidden * hidden_gradient, (1, 2))
    normalized_gradient = hidden_gradient * output_gain[:, None, None]
    first_average_term, second_average_term = lax.psum(
        (jnp.sum(normalized_gradient, 0), jnp.sum(normalized_gradient * normalized_hidden, 0)),
        "chan",
    )
    triangle_gradient = hidden_inverse_deviation * (
        normalized_gradient
        - first_average_term / HIDDEN_WIDTH
        - normalized_hidden * (second_average_term / HIDDEN_WIDTH)
    )
    d_tri_cols = lax.all_to_all(triangle_gradient, "row", split_axis=2, concat_axis=1, tiled=True)
    d_left = jnp.einsum("hrj,hjk->hrk", triangle_gradient, right_all, precision=hp)
    d_right = jnp.einsum(
        "hij,hik->hjk", d_tri_cols, lax.all_gather(left, "row", axis=1, tiled=True), precision=hp
    )
    d_proj = jnp.stack(
        [
            d_left * left_sig,
            d_left * proj[0] * left_sig * (1.0 - left_sig),
            d_right * right_sig,
            d_right * proj[2] * right_sig * (1.0 - right_sig),
        ]
    )
    g_edges = jnp.einsum("crn,ehrn->ech", normed, d_proj, precision=hp)
    g_gate = jnp.einsum("drn,crn->dc", normed, d_gate_pre, precision=hp)
    offset = lax.axis_index("chan") * shard_c
    first_part = jnp.einsum("ech,ehrn->crn", w_edges, d_proj, precision=hp)
    d_normed = lax.psum(
        first_part + jnp.einsum("dc,crn->drn", w_gate, d_gate_pre, precision=hp), "chan"
    )
    d_zhat = d_normed * in_gain[:, None, None]
    first_mean = jnp.mean(d_zhat, 0)
    second_mean = jnp.mean(d_zhat * zhat, 0)
    d_full = pair_rstd * (d_zhat - first_mean - zhat * second_mean)
    d_pair = lax.dynamic_slice_in_dim(d_full, offset, shard_c, 0)
    g_in_gain = lax.dynamic_slice_in_dim(jnp.sum(zhat * d_normed, (1, 2)), offset, shard_c, 0)
    totals = lax.psum((g_in_gain, output_gain_gradient, g_edges, g_gate, g_out), "row")
    return (update, d_pair, totals[0], totals[1], totals[2], totals[3], totals[4])


def split(x):
    hi = x.astype(BF16)
    return hi, (x - hi.astype(F32)).astype(BF16)


def dot(a, b):
    return jnp.dot(a, b, preferred_element_type=F32)


def put_split(ref, at, x):
    high, low = split(x)
    ref[at, :LANES], ref[at, LANES : 2 * LANES], ref[at, 2 * LANES :] = high, low, high


def down(a, b):
    return lax.dot_general(a, b, (((0,), (0,)), ((), ())), preferred_element_type=F32)


def chunks(cells, step=CHUNK):
    return [slice(at, at + step) for at in range(0, cells, step)]


def mean_lanes(x):
    return jnp.mean(x, axis=-1, keepdims=True)


def norm_lanes(x):
    centred = x - mean_lanes(x)
    rstd = lax.rsqrt(mean_lanes(centred * centred) + EPS)
    return centred * rstd, rstd


def cells_from(k, own_ref, rest_ref, blk):
    half = blk // 2
    across = own_ref.shape[1]
    low = (lax.broadcasted_iota(jnp.int32, (half, LANES), 1) < LANES // 2) == (lax.axis_index("chan") == 0)
    for t in range(2 * across // half):
        at = t * half % across

        def rest(line, at=at):
            return rest_ref[k, line * across + at : line * across + at + half, :]

        if t * half < across:
            own, other = own_ref[k, at : at + half, :], rest(2)
        else:
            own, other = rest(1), rest(0)
        yield jnp.where(low, own, other)
        yield pltpu.roll(jnp.where(low, other, own), LANES // 2, 1)


def true_row(p, q, upper, rows):
    row = lax.axis_index("row")
    far, t = p // (rows // 2), p % (rows // 2) // q
    return (((row // 2) ^ ((upper - t % upper) % upper * 2 + t // upper)) * 2 + ((row % 2) ^ far)) * q + p % q


def pack_kernel(we, wg, wo, gain, mine):
    s = wg.shape[0]
    for e in range(4):
        mine[e * s : (e + 1) * s, :] = we[e]
    mine[4 * s : 5 * s, :] = wg[...]
    mine[5 * s : 6 * s, :] = wo[...]
    mine[6 * s :, :] = gain[...]


def prepare_kernel(gain_ref, mine, other, wnh, wnl, wdh, woh, wqh, gain_out):
    c = LANES
    s = c // 2
    chan = lax.axis_index("chan")
    gain = gain_ref[...]

    def both(k):
        at = slice(k * s, (k + 1) * s)
        return mine[at, :], other[at, :]

    def put(k, whole):
        at = slice(k * c, (k + 1) * c)
        wnh[at, :], wnl[at, :] = split(whole)
        high, low = split(whole.T)
        wdh[:c, at], wdh[c : 2 * c, at], wdh[2 * c :, at] = high, high, low

    for e in range(4):
        put(e, jnp.concatenate(both(e), axis=0) * gain)
    a, b = both(4)
    put(4, jnp.concatenate([jnp.where(chan == 0, a, b), jnp.where(chan == 0, b, a)], axis=0) * gain)
    whole = jnp.concatenate(both(5), axis=0)
    high, low = split(whole)
    woh[:c, :], woh[c : 2 * c, :], woh[2 * c :, :] = high, high, low
    high, low = split(whole.T)
    wqh[:c, :], wqh[c : 2 * c, :], wqh[2 * c :, :] = high, high, low
    gain_out[:, :s] = mine[6 * s : 6 * s + 1, :s]
    gain_out[:, s:] = other[6 * s : 6 * s + 1, :s]


def project_kernel(blk, own_ref, rest_ref, wdh, z, left, s1, right, s3, gate, zown, rown, ct, proj):
    c = LANES
    half = blk // 2
    if ct is not None:
        for k, cells in enumerate(cells_from(1, own_ref, rest_ref, blk)):
            ct[k * half : (k + 1) * half, :] = cells
    for k, cells in enumerate(cells_from(0, own_ref, rest_ref, blk)):
        at = slice(k * half, (k + 1) * half)
        zhat, rstd = norm_lanes(cells)
        put_split(z, at, zhat)
        if k < 2 and zown is not None:
            zown[at, :] = zhat
            rown[at, :] = jnp.broadcast_to(rstd, zhat.shape)
    for at in chunks(z.shape[0], DEEP):
        proj[at, :] = dot(z[at, :], wdh[...])
    for at in chunks(z.shape[0]):
        a = jax.nn.sigmoid(proj[at, c : 2 * c])
        left[at, :], s1[at, :] = a * proj[at, :c], a
        a = jax.nn.sigmoid(proj[at, 3 * c : 4 * c])
        right[at, :], s3[at, :] = a * proj[at, 2 * c : 3 * c], a
        gate[at, :] = jax.nn.sigmoid(proj[at, 4 * c :])


def products(n, x_row, y_of):
    acc = [jnp.zeros((n // 8, 8, LANES), F32) for _ in range(ROWS)]
    for m in range(n):
        y = y_of(m).reshape(n // 8, 8, LANES)
        for a in range(ROWS):
            acc[a] = acc[a] + x_row(a, m)[None] * y
    return jnp.concatenate([part.reshape(n, LANES) for part in acc], axis=0)


def row_of(ref, at):
    return ref[pl.ds(at, 8, stride=0), :]


def over_rows(n, outs, bodies):
    def some(b, carry):
        here = pl.ds(pl.multiple_of(b * ROWS * n, ROWS * n), ROWS * n)
        for out, body in zip(outs, bodies, strict=True):
            out[here, :] = body(b * ROWS)
        return carry

    lax.fori_loop(0, n // ROWS, some, 0)


def triangle_kernel(n, q, upper, left, sides, gain_ref, woh, xhat, rstds, xs, mixed, right, right_t, tri):
    c = LANES
    for p in range(n):
        ref, at = sides[p // (n // 2)], p % (n // 2) * n
        right[pl.ds(pl.multiple_of(true_row(p, q, upper, n) * n, n), n), :] = ref[at : at + n, :]
    right_t[...] = jnp.swapaxes(right[...].reshape(n, n, c), 0, 1).reshape(n * n, c)

    def body(first):
        return products(
            n, lambda a, m: row_of(left, (first + a) * n + m), lambda m: right_t[m * n : (m + 1) * n, :]
        )

    over_rows(n, (tri,), (body,))
    for at in chunks(n * n):
        found, rstd = norm_lanes(tri[at, :])
        xhat[at, :] = found
        rstds[at, :] = jnp.broadcast_to(rstd, found.shape)
        put_split(xs, at, found * gain_ref[...])
    for at in chunks(n * n, DEEP):
        mixed[at, :] = dot(xs[at, :], woh[...])


def gradient_kernel(
    n, ct_n, far_a, far_b, left, right, z_n, s1_n, right_n, s3_n, gate_n, z_f, s1_f, right_f, s3_f, gate_f, zown, rown,
    xhat, rstds, xs, mixed, gain_ref, out_gain_ref, own, other, wnh, wnl, wqh,
    up_ref, dp_ref, dig_ref, dog_ref, de_ref, dg_ref, do_ref, ms, dh, dl, upd, hidden, dtri, d_left, d_right, grads,
):
    c, s = LANES, LANES // 2
    blk = up_ref.shape[0]
    q = blk // n
    upper = 2 * far_a.shape[1] // blk
    chan = lax.axis_index("chan")
    half = blk // 2
    part = n * n // 2
    near = (ct_n[at, :] for at in chunks(part, half))
    sides = ((near, gate_n), (cells_from(1, far_a, far_b, blk), gate_f))

    for k, (cells, gate) in enumerate(sides):
        for b, ct in enumerate(cells):
            here, there = slice(b * half, (b + 1) * half), slice(k * part + b * half, k * part + (b + 1) * half)
            a, mix = gate[here, :], mixed[there, :]
            dm = ct * a
            put_split(ms, there, dm)
            dh[there, 4 * c :], dl[there, 4 * c :] = split(dm * mix * (1.0 - a))
            if k == 0 and b < 2:
                upd[here, :] = a * mix
    for at in chunks(n * n, DEEP):
        hidden[at, :] = dot(ms[at, :], wqh[...])
    total = jnp.zeros((8, c), F32)
    for at in chunks(n * n):
        found, ng = xhat[at, :], hidden[at, :] * out_gain_ref[...]
        dtri[at, :] = rstds[at, :] * (ng - mean_lanes(ng) - found * mean_lanes(ng * found))
        total = total + jnp.sum((found * hidden[at, :]).reshape(-1, 8, c), axis=0)
    dog_ref[...] = jnp.sum(total, axis=0, keepdims=True)[:, :s]

    def of_left(first):
        return products(n, lambda a, m: row_of(dtri, (first + a) * n + m), lambda m: right[m * n : (m + 1) * n, :])

    def of_right(first):
        mine = [true_row(first + a, q, upper, n) for a in range(ROWS)]
        return products(n, lambda a, m: row_of(dtri, m * n + mine[a]), lambda m: left[m * n : (m + 1) * n, :])

    over_rows(n, (d_left, d_right), (of_left, of_right))
    for k, (s1, edge, s3) in enumerate(((s1_n, right_n, s3_n), (s1_f, right_f, s3_f))):
        for here in chunks(part):
            at = slice(k * part + here.start, k * part + here.stop)
            d, a = d_left[at, :], s1[here, :]
            dh[at, :c], dl[at, :c] = split(d * a)
            dh[at, c : 2 * c], dl[at, c : 2 * c] = split(d * left[at, :] * (1.0 - a))
            d, a = d_right[at, :], s3[here, :]
            dh[at, 2 * c : 3 * c], dl[at, 2 * c : 3 * c] = split(d * a)
            dh[at, 3 * c : 4 * c], dl[at, 3 * c : 4 * c] = split(d * edge[here, :] * (1.0 - a))

    def turned(at, z):
        zt = z[:, : 2 * c].T
        wide = dot(zt, dh[at, :])
        return wide[:c] + (wide[c:] + dot(zt[:c], dl[at, :]))

    def joined(high, low, b):
        wide = down(high, b)
        return wide[:, :c] + (wide[:, c:] + down(low, b[:, :c]))

    grads[...] = (turned(slice(0, part), z_n) + turned(slice(part, 2 * part), z_f)).T
    do_ref[...] = joined(xs[:, :s], xs[:, c : c + s], ms[:, : 2 * c])

    gain = gain_ref[...]
    mine = pl.ds(pl.multiple_of(4 * c + s * chan, s), s)
    others = pl.ds(pl.multiple_of(4 * c + s * (1 - chan), s), s)
    dg_ref[...] = grads[mine, :] * gain
    weighted = own[4 * s : 5 * s, :] * grads[mine, :] + other[4 * s : 5 * s, :] * grads[others, :]
    for e in range(4):
        mine, others = grads[e * c : e * c + s, :], grads[e * c + s : (e + 1) * c, :]
        de_ref[e] = mine * gain
        at = slice(e * s, (e + 1) * s)
        weighted = weighted + own[at, :] * mine + other[at, :] * others
    d_gain = jnp.sum(weighted, axis=0, keepdims=True)

    def own_half(x):
        return jnp.where(chan == 0, x[:, :s], pltpu.roll(x, s, 1)[:, :s])

    dig_ref[...] = own_half(jnp.broadcast_to(d_gain, (8, c)))[:1]
    up_ref[...] = own_half(upd[...])
    dz = dot(dh[:blk, :], wnh[...]) + (dot(dh[:blk, :], wnl[...]) + dot(dl[:blk, :], wnh[...]))
    zhat = zown[...]
    dp_ref[...] = own_half(rown[...] * (dz - mean_lanes(dz) - zhat * mean_lanes(dz * zhat)))


def rest_kernel(
    n, blk, far_a, far_b, z_n, left_n, s1_n, right_n, s3_n, gate_n, zown, rown, ct_n, gain_ref, out_gain_ref, own,
    other, wnh, wnl, wdh, woh, wqh, up_ref, dp_ref, dig_ref, dog_ref, de_ref, dg_ref, do_ref,
    left, right, z_f, s1_f, right_f, s3_f, gate_f, xhat, rstds, xs, mixed, right_t, tri, proj, *scratch,
):
    q, upper, part = blk // n, 2 * far_a.shape[1] // blk, n * n // 2
    left[:part, :] = left_n[...]
    left_f = left.at[pl.ds(part, part)]
    project_kernel(blk, far_a, far_b, wdh, z_f, left_f, s1_f, right_f, s3_f, gate_f, None, None, None, proj)
    sides = (right_n, right_f)
    triangle_kernel(n, q, upper, left, sides, out_gain_ref, woh, xhat, rstds, xs, mixed, right, right_t, tri)
    gradient_kernel(
        n, ct_n, far_a, far_b, left, right, z_n, s1_n, right_n, s3_n, gate_n, z_f, s1_f, right_f, s3_f, gate_f, zown, rown,
        xhat, rstds, xs, mixed, gain_ref, out_gain_ref, own, other, wnh, wnl, wqh,
        up_ref, dp_ref, dig_ref, dog_ref, de_ref, dg_ref, do_ref, *scratch,
    )


def call(kernel, name, out, scratch, limit, flops, *args):
    vm = pl.BlockSpec(memory_space=pltpu.VMEM)
    return pl.pallas_call(
        kernel,
        out_shape=[jax.ShapeDtypeStruct(shape, dtype) for shape, dtype in out],
        in_specs=[vm] * len(args),
        out_specs=[vm] * len(out),
        scratch_shapes=[pltpu.VMEM(shape, dtype) for shape, dtype in scratch],
        compiler_params=pltpu.CompilerParams(vmem_limit_bytes=limit << 20),
        cost_estimate=pl.CostEstimate(flops=flops, bytes_accessed=1 << 10, transcendentals=0),
        name=name,
    )(*args)


def gathered(devices, pair, in_gain, output_gain, w_edges, w_gate, w_out, cotangent):
    s, q, n = pair.shape
    c = 2 * s
    blk = q * n
    cells = n * n
    upper = devices // 8

    def swap(x, bits):
        return lax.ppermute(x, ("row", "chan"), [(i, i ^ bits) for i in range(devices)])

    def packed(x):
        x = jnp.transpose(x, (1, 2, 0)).reshape(2, blk // 2, s)
        return jnp.concatenate([x[0], x[1]], axis=1)[None]

    w_e = jnp.transpose(w_edges, (0, 2, 1))
    w_g = jnp.transpose(w_gate)
    held = jnp.concatenate([packed(pair), packed(cotangent)])
    gain_row = jnp.pad(output_gain[None], ((0, 7), (0, s)))
    held = lax.optimization_barrier(held)
    held = jnp.where(lax.axis_index("chan") == 0, held, jnp.concatenate([held[..., s:], held[..., :s]], axis=-1))
    (mine,) = call(pack_kernel, "pack", [((6 * s + 8, c), F32)], [], 8, 1 << 20, w_e, w_g, w_out, gain_row)
    held = jnp.concatenate([held] + [swap(held, 8 * apart) for apart in range(upper - 1, 0, -1)], axis=1)
    other = swap(mine, 1)
    held, mine = lax.optimization_barrier((held, mine))
    parts = [swap(held, bits) for bits in (5, 4, 1)]

    gain = in_gain[None]
    wnh, wnl, wdh, woh, wqh, out_gain = call(
        prepare_kernel,
        "prepare",
        [(x, BF16) for x in [(5 * c, c), (5 * c, c), (3 * c, 5 * c), (3 * c, c), (3 * c, c)]]
        + [((1, c), F32)],
        [],
        8,
        1 << 20,
        gain, mine, other,
    )
    far_a = swap(held, 2)
    parts, wdh, far_a = lax.optimization_barrier((parts, wdh, far_a))
    others = jnp.concatenate(parts, axis=1)
    far_b = swap(others, 2)

    full, both, wide = ((cells, c), F32), ((cells, 3 * c), BF16), ((cells, 5 * c), BF16)
    part, own = ((cells // 2, c), F32), ((blk, c), F32)
    half, many = [((cells // 2, 3 * c), BF16)] + [part] * 5, ((cells // 2, 5 * c), F32)
    near = call(
        functools.partial(project_kernel, blk), "project", half + [own] * 2 + [part], [many], 16, 1 << 30, held, others, wdh
    )
    up, dp, dig, dog, de, dg, do = call(
        functools.partial(rest_kernel, n, blk),
        "rest",
        [(x, F32) for x in [(blk, s), (blk, s), (1, s), (1, s), (4, s, c), (s, c), (s, c)]],
        [full, full] + half[:1] + [part] * 4 + [full, full, both, full, full, full, many]
        + [both, wide, wide, own] + [full] * 4 + [((5 * c, c), F32)],
        32,
        1 << 33,
        far_a, far_b, *near, gain, out_gain, mine, other, wnh, wnl, wdh, woh, wqh,
    )

    def pair_of(x):
        return jnp.transpose(x.reshape(q, n, s), (2, 0, 1))

    return (pair_of(up), pair_of(dp), dig[0], dog[0], jnp.transpose(de, (0, 2, 1)), jnp.transpose(dg), do)


def solution(mesh):
    devices, chans = mesh.size, mesh.shape["chan"]

    def shards(pair, in_gain, output_gain, w_edges, *rest):
        n, c = pair.shape[2], w_edges.shape[1]
        fits = (
            chans == 2 and devices >= 8 and devices & (devices - 1) == 0 and n <= 32 and n * n % (2 * DEEP) == 0 and n % ROWS == 0
            and c == LANES and w_edges.shape[2] * chans == LANES and (pair.shape[1] * n) % 32 == 0
        )
        step = functools.partial(gathered, devices) if fits else spread
        return step(pair, in_gain, output_gain, w_edges, *rest)

    placed = (
        P("chan", "row", None),
        P(),
        P("chan"),
        P(None, None, "chan"),
        P(None, "chan"),
        P("chan", None),
        P("chan", "row", None),
    )
    return jax.shard_map(
        shards,
        mesh=mesh,
        in_specs=placed,
        out_specs=(placed[0], placed[0], P("chan"), P("chan"), placed[3], placed[4], placed[5]),
        check_vma=False,
    )
```

```python
import functools

import jax
import jax.numpy as jnp
from jax import lax
from jax.experimental import pallas as pl
from jax.experimental.pallas import tpu as pltpu
from jax.sharding import PartitionSpec as P

HIDDEN_WIDTH = 128
EPS = 1e-05
F32 = jnp.float32
BF16 = jnp.bfloat16
LANES = 128
ROWS = 16
CHUNK = 64
DEEP = 256


def spread(pair, in_gain, output_gain, w_edges, w_gate, w_out, cotangent):
    hp = lax.Precision.HIGHEST
    shard_c = pair.shape[0]
    whole = lax.all_gather(pair, "chan", axis=0, tiled=True)
    centred = whole - jnp.mean(whole, 0)
    pair_rstd = lax.rsqrt(jnp.mean(centred * centred, 0) + 1e-05)
    zhat = centred * pair_rstd
    normed = zhat * in_gain[:, None, None]
    proj = jnp.einsum("ech,crn->ehrn", w_edges, normed, precision=hp)
    left_sig = jax.nn.sigmoid(proj[1])
    left = left_sig * proj[0]
    right_sig = jax.nn.sigmoid(proj[3])
    right = right_sig * proj[2]
    gate = jax.nn.sigmoid(jnp.einsum("dc,drn->crn", w_gate, normed, precision=hp))
    right_all = lax.all_gather(right, "row", axis=1, tiled=True)
    triangle_product = jnp.einsum("hrk,hjk->hrj", left, right_all, precision=hp)
    first, second = lax.psum(
        (jnp.sum(triangle_product, 0), jnp.sum(triangle_product * triangle_product, 0)), "chan"
    )
    hidden_average = first / HIDDEN_WIDTH
    hidden_inverse_deviation = lax.rsqrt(
        second / HIDDEN_WIDTH - hidden_average * hidden_average + 1e-05
    )
    normalized_hidden = (triangle_product - hidden_average) * hidden_inverse_deviation
    hidden_state = normalized_hidden * output_gain[:, None, None]
    mixed = lax.psum_scatter(
        jnp.einsum("hc,hrn->crn", w_out, hidden_state, precision=hp),
        "chan",
        scatter_dimension=0,
        tiled=True,
    )
    update = gate * mixed
    d_mixed = cotangent * gate
    d_gate_pre = cotangent * mixed * gate * (1.0 - gate)
    d_mixed_all = lax.all_gather(d_mixed, "chan", axis=0, tiled=True)
    hidden_gradient = jnp.einsum("hc,crn->hrn", w_out, d_mixed_all, precision=hp)
    g_out = jnp.einsum("hrn,crn->hc", hidden_state, d_mixed_all, precision=hp)
    output_gain_gradient = jnp.sum(normalized_hidden * hidden_gradient, (1, 2))
    normalized_gradient = hidden_gradient * output_gain[:, None, None]
    first_average_term, second_average_term = lax.psum(
        (jnp.sum(normalized_gradient, 0), jnp.sum(normalized_gradient * normalized_hidden, 0)),
        "chan",
    )
    triangle_gradient = hidden_inverse_deviation * (
        normalized_gradient
        - first_average_term / HIDDEN_WIDTH
        - normalized_hidden * (second_average_term / HIDDEN_WIDTH)
    )
    d_tri_cols = lax.all_to_all(triangle_gradient, "row", split_axis=2, concat_axis=1, tiled=True)
    d_left = jnp.einsum("hrj,hjk->hrk", triangle_gradient, right_all, precision=hp)
    d_right = jnp.einsum(
        "hij,hik->hjk", d_tri_cols, lax.all_gather(left, "row", axis=1, tiled=True), precision=hp
    )
    d_proj = jnp.stack(
        [
            d_left * left_sig,
            d_left * proj[0] * left_sig * (1.0 - left_sig),
            d_right * right_sig,
            d_right * proj[2] * right_sig * (1.0 - right_sig),
        ]
    )
    g_edges = jnp.einsum("crn,ehrn->ech", normed, d_proj, precision=hp)
    g_gate = jnp.einsum("drn,crn->dc", normed, d_gate_pre, precision=hp)
    offset = lax.axis_index("chan") * shard_c
    first_part = jnp.einsum("ech,ehrn->crn", w_edges, d_proj, precision=hp)
    d_normed = lax.psum(
        first_part + jnp.einsum("dc,crn->drn", w_gate, d_gate_pre, precision=hp), "chan"
    )
    d_zhat = d_normed * in_gain[:, None, None]
    first_mean = jnp.mean(d_zhat, 0)
    second_mean = jnp.mean(d_zhat * zhat, 0)
    d_full = pair_rstd * (d_zhat - first_mean - zhat * second_mean)
    d_pair = lax.dynamic_slice_in_dim(d_full, offset, shard_c, 0)
    g_in_gain = lax.dynamic_slice_in_dim(jnp.sum(zhat * d_normed, (1, 2)), offset, shard_c, 0)
    totals = lax.psum((g_in_gain, output_gain_gradient, g_edges, g_gate, g_out), "row")
    return (update, d_pair, totals[0], totals[1], totals[2], totals[3], totals[4])


def split(x):
    hi = x.astype(BF16)
    return hi, (x - hi.astype(F32)).astype(BF16)


def dot(a, b):
    return jnp.dot(a, b, preferred_element_type=F32)


def put_split(ref, at, x):
    high, low = split(x)
    ref[at, :LANES], ref[at, LANES : 2 * LANES], ref[at, 2 * LANES :] = high, low, high


def down(a, b):
    return lax.dot_general(a, b, (((0,), (0,)), ((), ())), preferred_element_type=F32)


def chunks(cells, step=CHUNK):
    return [slice(at, at + step) for at in range(0, cells, step)]


def mean_lanes(x):
    return jnp.mean(x, axis=-1, keepdims=True)


def norm_lanes(x):
    centred = x - mean_lanes(x)
    rstd = lax.rsqrt(mean_lanes(centred * centred) + EPS)
    return centred * rstd, rstd


def cells_from(k, own_ref, cross_ref, rest_ref, blk):
    half = blk // 2
    across = own_ref.shape[1]
    low = (lax.broadcasted_iota(jnp.int32, (half, LANES), 1) < LANES // 2) == (lax.axis_index("chan") == 0)
    for t in range(2 * across // half):
        at = t * half % across

        def rest(line, at=at):
            return rest_ref[k, line * across + at : line * across + at + half, :]

        if t * half < across:
            own, other = own_ref[k, at : at + half, :], rest(1)
        else:
            own, other = rest(0), cross_ref[k, at : at + half, :]
        yield jnp.where(low, own, other)
        yield pltpu.roll(jnp.where(low, other, own), LANES // 2, 1)


def true_row(p, q, upper, rows):
    row = lax.axis_index("row")
    far, t = p // (rows // 2), p % (rows // 2) // q
    return (((row // 2) ^ ((upper - t % upper) % upper * 2 + t // upper)) * 2 + ((row % 2) ^ far)) * q + p % q


def pack_kernel(we, wg, wo, gain, mine):
    s = wg.shape[0]
    for e in range(4):
        mine[e * s : (e + 1) * s, :] = we[e]
    mine[4 * s : 5 * s, :] = wg[...]
    mine[5 * s : 6 * s, :] = wo[...]
    mine[6 * s :, :] = gain[...]


def prepare_kernel(gain_ref, mine, other, wnh, wnl, wdh, woh, wqh, gain_out):
    c = LANES
    s = c // 2
    chan = lax.axis_index("chan")
    gain = gain_ref[...]

    def both(k):
        at = slice(k * s, (k + 1) * s)
        return mine[at, :], other[at, :]

    def put(k, whole):
        at = slice(k * c, (k + 1) * c)
        wnh[at, :], wnl[at, :] = split(whole)
        high, low = split(whole.T)
        wdh[:c, at], wdh[c : 2 * c, at], wdh[2 * c :, at] = high, high, low

    for e in range(4):
        put(e, jnp.concatenate(both(e), axis=0) * gain)
    a, b = both(4)
    put(4, jnp.concatenate([jnp.where(chan == 0, a, b), jnp.where(chan == 0, b, a)], axis=0) * gain)
    whole = jnp.concatenate(both(5), axis=0)
    high, low = split(whole)
    woh[:c, :], woh[c : 2 * c, :], woh[2 * c :, :] = high, high, low
    high, low = split(whole.T)
    wqh[:c, :], wqh[c : 2 * c, :], wqh[2 * c :, :] = high, high, low
    gain_out[:, :s] = mine[6 * s : 6 * s + 1, :s]
    gain_out[:, s:] = other[6 * s : 6 * s + 1, :s]


def project_kernel(blk, own_ref, cross_ref, rest_ref, wdh, z, left, s1, right, s3, gate, zown, rown, ct, proj):
    c = LANES
    half = blk // 2
    if ct is not None:
        for k, cells in enumerate(cells_from(1, own_ref, cross_ref, rest_ref, blk)):
            ct[k * half : (k + 1) * half, :] = cells
    for k, cells in enumerate(cells_from(0, own_ref, cross_ref, rest_ref, blk)):
        at = slice(k * half, (k + 1) * half)
        zhat, rstd = norm_lanes(cells)
        put_split(z, at, zhat)
        if k < 2 and zown is not None:
            zown[at, :] = zhat
            rown[at, :] = jnp.broadcast_to(rstd, zhat.shape)
    for at in chunks(z.shape[0], DEEP):
        proj[at, :] = dot(z[at, :], wdh[...])
    for at in chunks(z.shape[0]):
        a = jax.nn.sigmoid(proj[at, c : 2 * c])
        left[at, :], s1[at, :] = a * proj[at, :c], a
        a = jax.nn.sigmoid(proj[at, 3 * c : 4 * c])
        right[at, :], s3[at, :] = a * proj[at, 2 * c : 3 * c], a
        gate[at, :] = jax.nn.sigmoid(proj[at, 4 * c :])


def products(n, x_row, y_of):
    acc = [jnp.zeros((n // 8, 8, LANES), F32) for _ in range(ROWS)]
    for m in range(n):
        y = y_of(m).reshape(n // 8, 8, LANES)
        for a in range(ROWS):
            acc[a] = acc[a] + x_row(a, m)[None] * y
    return jnp.concatenate([part.reshape(n, LANES) for part in acc], axis=0)


def row_of(ref, at):
    return ref[pl.ds(at, 8, stride=0), :]


def over_rows(n, outs, bodies):
    def some(b, carry):
        here = pl.ds(pl.multiple_of(b * ROWS * n, ROWS * n), ROWS * n)
        for out, body in zip(outs, bodies, strict=True):
            out[here, :] = body(b * ROWS)
        return carry

    lax.fori_loop(0, n // ROWS, some, 0)


def triangle_kernel(n, q, upper, left, sides, gain_ref, woh, xhat, rstds, xs, mixed, right, right_t, tri):
    c = LANES
    for p in range(n):
        ref, at = sides[p // (n // 2)], p % (n // 2) * n
        right[pl.ds(pl.multiple_of(true_row(p, q, upper, n) * n, n), n), :] = ref[at : at + n, :]
    right_t[...] = jnp.swapaxes(right[...].reshape(n, n, c), 0, 1).reshape(n * n, c)

    def body(first):
        return products(
            n, lambda a, m: row_of(left, (first + a) * n + m), lambda m: right_t[m * n : (m + 1) * n, :]
        )

    over_rows(n, (tri,), (body,))
    for at in chunks(n * n):
        found, rstd = norm_lanes(tri[at, :])
        xhat[at, :] = found
        rstds[at, :] = jnp.broadcast_to(rstd, found.shape)
        put_split(xs, at, found * gain_ref[...])
    for at in chunks(n * n, DEEP):
        mixed[at, :] = dot(xs[at, :], woh[...])


def gradient_kernel(
    n, ct_n, far_a, far_c, far_b, left, right, z_n, s1_n, right_n, s3_n, gate_n, z_f, s1_f, right_f, s3_f, gate_f, zown, rown,
    xhat, rstds, xs, mixed, gain_ref, out_gain_ref, own, other, wnh, wnl, wqh,
    up_ref, dp_ref, dig_ref, dog_ref, de_ref, dg_ref, do_ref, ms, dh, dl, upd, hidden, dtri, d_left, d_right, grads,
):
    c, s = LANES, LANES // 2
    blk = up_ref.shape[0]
    q = blk // n
    upper = 2 * far_a.shape[1] // blk
    chan = lax.axis_index("chan")
    half = blk // 2
    part = n * n // 2
    near = (ct_n[at, :] for at in chunks(part, half))
    sides = ((near, gate_n), (cells_from(1, far_a, far_c, far_b, blk), gate_f))

    for k, (cells, gate) in enumerate(sides):
        for b, ct in enumerate(cells):
            here, there = slice(b * half, (b + 1) * half), slice(k * part + b * half, k * part + (b + 1) * half)
            a, mix = gate[here, :], mixed[there, :]
            dm = ct * a
            put_split(ms, there, dm)
            dh[there, 4 * c :], dl[there, 4 * c :] = split(dm * mix * (1.0 - a))
            if k == 0 and b < 2:
                upd[here, :] = a * mix
    for at in chunks(n * n, DEEP):
        hidden[at, :] = dot(ms[at, :], wqh[...])
    total = jnp.zeros((8, c), F32)
    for at in chunks(n * n):
        found, ng = xhat[at, :], hidden[at, :] * out_gain_ref[...]
        dtri[at, :] = rstds[at, :] * (ng - mean_lanes(ng) - found * mean_lanes(ng * found))
        total = total + jnp.sum((found * hidden[at, :]).reshape(-1, 8, c), axis=0)
    dog_ref[...] = jnp.sum(total, axis=0, keepdims=True)[:, :s]

    def of_left(first):
        return products(n, lambda a, m: row_of(dtri, (first + a) * n + m), lambda m: right[m * n : (m + 1) * n, :])

    def of_right(first):
        mine = [true_row(first + a, q, upper, n) for a in range(ROWS)]
        return products(n, lambda a, m: row_of(dtri, m * n + mine[a]), lambda m: left[m * n : (m + 1) * n, :])

    over_rows(n, (d_left, d_right), (of_left, of_right))
    for k, (s1, edge, s3) in enumerate(((s1_n, right_n, s3_n), (s1_f, right_f, s3_f))):
        for here in chunks(part):
            at = slice(k * part + here.start, k * part + here.stop)
            d, a = d_left[at, :], s1[here, :]
            dh[at, :c], dl[at, :c] = split(d * a)
            dh[at, c : 2 * c], dl[at, c : 2 * c] = split(d * left[at, :] * (1.0 - a))
            d, a = d_right[at, :], s3[here, :]
            dh[at, 2 * c : 3 * c], dl[at, 2 * c : 3 * c] = split(d * a)
            dh[at, 3 * c : 4 * c], dl[at, 3 * c : 4 * c] = split(d * edge[here, :] * (1.0 - a))

    def turned(at, z):
        zt = z[:, : 2 * c].T
        wide = dot(zt, dh[at, :])
        return wide[:c] + (wide[c:] + dot(zt[:c], dl[at, :]))

    def joined(high, low, b):
        wide = down(high, b)
        return wide[:, :c] + (wide[:, c:] + down(low, b[:, :c]))

    grads[...] = (turned(slice(0, part), z_n) + turned(slice(part, 2 * part), z_f)).T
    do_ref[...] = joined(xs[:, :s], xs[:, c : c + s], ms[:, : 2 * c])

    gain = gain_ref[...]
    mine = pl.ds(pl.multiple_of(4 * c + s * chan, s), s)
    others = pl.ds(pl.multiple_of(4 * c + s * (1 - chan), s), s)
    dg_ref[...] = grads[mine, :] * gain
    weighted = own[4 * s : 5 * s, :] * grads[mine, :] + other[4 * s : 5 * s, :] * grads[others, :]
    for e in range(4):
        mine, others = grads[e * c : e * c + s, :], grads[e * c + s : (e + 1) * c, :]
        de_ref[e] = mine * gain
        at = slice(e * s, (e + 1) * s)
        weighted = weighted + own[at, :] * mine + other[at, :] * others
    d_gain = jnp.sum(weighted, axis=0, keepdims=True)

    def own_half(x):
        return jnp.where(chan == 0, x[:, :s], pltpu.roll(x, s, 1)[:, :s])

    dig_ref[...] = own_half(jnp.broadcast_to(d_gain, (8, c)))[:1]
    up_ref[...] = own_half(upd[...])
    dz = dot(dh[:blk, :], wnh[...]) + (dot(dh[:blk, :], wnl[...]) + dot(dl[:blk, :], wnh[...]))
    zhat = zown[...]
    dp_ref[...] = own_half(rown[...] * (dz - mean_lanes(dz) - zhat * mean_lanes(dz * zhat)))


def rest_kernel(
    n, blk, far_a, far_c, far_b, z_n, left_n, s1_n, right_n, s3_n, gate_n, zown, rown, ct_n, gain_ref, out_gain_ref, own,
    other, wnh, wnl, wdh, woh, wqh, up_ref, dp_ref, dig_ref, dog_ref, de_ref, dg_ref, do_ref,
    left, right, z_f, s1_f, right_f, s3_f, gate_f, xhat, rstds, xs, mixed, right_t, tri, proj, *scratch,
):
    q, upper, part = blk // n, 2 * far_a.shape[1] // blk, n * n // 2
    left[:part, :] = left_n[...]
    left_f = left.at[pl.ds(part, part)]
    project_kernel(blk, far_a, far_c, far_b, wdh, z_f, left_f, s1_f, right_f, s3_f, gate_f, None, None, None, proj)
    sides = (right_n, right_f)
    triangle_kernel(n, q, upper, left, sides, out_gain_ref, woh, xhat, rstds, xs, mixed, right, right_t, tri)
    gradient_kernel(
        n, ct_n, far_a, far_c, far_b, left, right, z_n, s1_n, right_n, s3_n, gate_n, z_f, s1_f, right_f, s3_f, gate_f, zown, rown,
        xhat, rstds, xs, mixed, gain_ref, out_gain_ref, own, other, wnh, wnl, wqh,
        up_ref, dp_ref, dig_ref, dog_ref, de_ref, dg_ref, do_ref, *scratch,
    )


def call(kernel, name, out, scratch, limit, flops, *args):
    vm = pl.BlockSpec(memory_space=pltpu.VMEM)
    return pl.pallas_call(
        kernel,
        out_shape=[jax.ShapeDtypeStruct(shape, dtype) for shape, dtype in out],
        in_specs=[vm] * len(args),
        out_specs=[vm] * len(out),
        scratch_shapes=[pltpu.VMEM(shape, dtype) for shape, dtype in scratch],
        compiler_params=pltpu.CompilerParams(vmem_limit_bytes=limit << 20),
        cost_estimate=pl.CostEstimate(flops=flops, bytes_accessed=1 << 10, transcendentals=0),
        name=name,
    )(*args)


def gathered(devices, pair, in_gain, output_gain, w_edges, w_gate, w_out, cotangent):
    s, q, n = pair.shape
    c = 2 * s
    blk = q * n
    cells = n * n
    upper = devices // 8

    def swap(x, bits):
        return lax.ppermute(x, ("row", "chan"), [(i, i ^ bits) for i in range(devices)])

    def packed(x):
        x = jnp.transpose(x, (1, 2, 0)).reshape(2, blk // 2, s)
        return jnp.concatenate([x[0], x[1]], axis=1)[None]

    w_e = jnp.transpose(w_edges, (0, 2, 1))
    w_g = jnp.transpose(w_gate)
    held = jnp.concatenate([packed(pair), packed(cotangent)])
    gain_row = jnp.pad(output_gain[None], ((0, 7), (0, s)))
    held = lax.optimization_barrier(held)
    held = jnp.where(lax.axis_index("chan") == 0, held, jnp.concatenate([held[..., s:], held[..., :s]], axis=-1))
    (mine,) = call(pack_kernel, "pack", [((6 * s + 8, c), F32)], [], 8, 1 << 20, w_e, w_g, w_out, gain_row)
    held = jnp.concatenate([held] + [swap(held, 8 * apart) for apart in range(upper - 1, 0, -1)], axis=1)
    other = swap(mine, 1)
    held, mine = lax.optimization_barrier((held, mine))
    parts = [swap(held, bits) for bits in (5, 4, 1)]

    gain = in_gain[None]
    wnh, wnl, wdh, woh, wqh, out_gain = call(
        prepare_kernel,
        "prepare",
        [(x, BF16) for x in [(5 * c, c), (5 * c, c), (3 * c, 5 * c), (3 * c, c), (3 * c, c)]]
        + [((1, c), F32)],
        [],
        8,
        1 << 20,
        gain, mine, other,
    )
    far_a = swap(held, 2)
    cross, *parts = parts
    far_c = swap(cross, 2)
    cross, parts, wdh, far_a = lax.optimization_barrier((cross, parts, wdh, far_a))
    others = jnp.concatenate(parts, axis=1)
    far_b = swap(others, 2)

    full, both, wide = ((cells, c), F32), ((cells, 3 * c), BF16), ((cells, 5 * c), BF16)
    part, own = ((cells // 2, c), F32), ((blk, c), F32)
    half, many = [((cells // 2, 3 * c), BF16)] + [part] * 5, ((cells // 2, 5 * c), F32)
    near = call(
        functools.partial(project_kernel, blk), "project", half + [own] * 2 + [part], [many], 16, 1 << 30, held, cross, others, wdh
    )
    up, dp, dig, dog, de, dg, do = call(
        functools.partial(rest_kernel, n, blk),
        "rest",
        [(x, F32) for x in [(blk, s), (blk, s), (1, s), (1, s), (4, s, c), (s, c), (s, c)]],
        [full, full] + half[:1] + [part] * 4 + [full, full, both, full, full, full, many]
        + [both, wide, wide, own] + [full] * 4 + [((5 * c, c), F32)],
        32,
        1 << 33,
        far_a, far_c, far_b, *near, gain, out_gain, mine, other, wnh, wnl, wdh, woh, wqh,
    )

    def pair_of(x):
        return jnp.transpose(x.reshape(q, n, s), (2, 0, 1))

    return (pair_of(up), pair_of(dp), dig[0], dog[0], jnp.transpose(de, (0, 2, 1)), jnp.transpose(dg), do)


def solution(mesh):
    devices, chans = mesh.size, mesh.shape["chan"]

    def shards(pair, in_gain, output_gain, w_edges, *rest):
        n, c = pair.shape[2], w_edges.shape[1]
        fits = (
            chans == 2 and devices >= 8 and devices & (devices - 1) == 0 and n <= 32 and n * n % (2 * DEEP) == 0 and n % ROWS == 0
            and c == LANES and w_edges.shape[2] * chans == LANES and (pair.shape[1] * n) % 32 == 0
        )
        step = functools.partial(gathered, devices) if fits else spread
        return step(pair, in_gain, output_gain, w_edges, *rest)

    placed = (
        P("chan", "row", None),
        P(),
        P("chan"),
        P(None, None, "chan"),
        P(None, "chan"),
        P("chan", None),
        P("chan", "row", None),
    )
    return jax.shard_map(
        shards,
        mesh=mesh,
        in_specs=placed,
        out_specs=(placed[0], placed[0], P("chan"), P("chan"), placed[3], placed[4], placed[5]),
        check_vma=False,
    )
```
